32 devices in a mesh: blk: 8 (over z, y), rows: 4 (over x, core).
Axes of the slice: x: 2, y: 2, z: 4, core: 2. Of those that a mesh axis runs over, the one named last changes fastest.
Arguments:
- start_block: float32 [64, 16384], P(None, ('rows', 'blk')), may hold values from -110 to 110, as said below
- tile_vals: float32 [2048, 128, 128], P(('rows', 'blk')), may hold values from 0 to 1, as said below
- tile_rows: int32 [2048], P(('rows', 'blk')), may hold values from 0 to 127, as said below
- tile_cols: int32 [2048], P(('rows', 'blk')), may hold values from 0 to 127, as said below
- tile_count: int32 [4, 8], P('rows', 'blk'), may hold values from 4 to 64, as said below
Outputs:
- spectral_basis: float32 [64, 16384], P(None, ('rows', 'blk'))
The draws below stay inside these ranges and needn't reach their ends.
Inputs may be any that keep to these rules, and one draw needn't show every extreme that they name: `start_block`: entries are finite. `tile_vals`: most entries are zero. In a slot s < 4 of a device every entry with |a - c| = 1 is positive. `tile_rows`: slot s < 4 of the device with blk index b in row group g has block row g * 32 + b * 4 + s; every other slot of row group g has a block row of that group. `tile_cols`: slot s < 4 of a device has block column equal to its block row. A slot of row group g has a block column in [g * 32 - 8, (g + 1) * 32 + 8) within the grid; both ends of that range occur on every device. `tile_count`: some device has 64 live slots and some device 4.
All inputs are finite; a program needn't handle non-finite values.
Results may differ from the reference program's by a relative error of at most 0.00012.
Values sent between devices are 32-bit elements; how exact they have to be, the bound alone decides.
No kernel may reach another device: no remote copies, remote signals or barrier semaphores. Data moves between devices by JAX's collectives and lax.ppermute only.
A program may use at most 64 MiB of HBM per device.

```python
import jax
import jax.numpy as jnp
from jax import lax

TILE = 128
K = 64
RB_DEV = 4
STEPS = 3
TILES_DEV = 64
GB = 32
REACH = 8
NBLOCKS = 128
ROWS_ALL = 16384
N_BLK = 8
N_ROWS = 4


def draw_start_block(key, part):
    key_a = jax.random.fold_in(key, 11)
    key_b = jax.random.fold_in(key, 12)
    base_draw = jnp.clip(jax.random.normal(key_a, (K, ROWS_ALL), jnp.float32), -6.0, 6.0)
    column_scale = jnp.exp(jax.random.uniform(key_b, (K, 1), jnp.float32) * jnp.log(10.0))
    position = jnp.arange(ROWS_ALL, dtype=jnp.float32)[None, :] / ROWS_ALL
    return base_draw * column_scale * jnp.sqrt(1.0 + 2.0 * position)


def draw_tile_vals(key, part):
    slot_total = N_ROWS * N_BLK * TILES_DEV
    slot = (jnp.arange(slot_total, dtype=jnp.int32) % TILES_DEV)[:, None, None]
    row_pos = jnp.arange(TILE, dtype=jnp.int32)[None, :, None]
    col_pos = jnp.arange(TILE, dtype=jnp.int32)[None, None, :]
    spacing = jnp.abs(row_pos - col_pos)
    coin = jax.random.uniform(jax.random.fold_in(key, 51), (slot_total, TILE, TILE), jnp.float32)
    band = (spacing == 1) | (spacing >= 2) & (spacing <= 6) & (coin < 0.6)
    sparse = coin < 0.012
    chosen = jnp.where(slot < RB_DEV, band, sparse)
    value_key = jax.random.fold_in(key, 52)
    values = 0.02 * jnp.exp(jax.random.uniform(value_key, (slot_total, TILE, TILE), jnp.float32) * jnp.log(50.0))
    return jnp.where(chosen, values, 0.0)


def slot_layout():
    slot_ids = jnp.arange(N_ROWS * N_BLK * TILES_DEV, dtype=jnp.int32)
    device = slot_ids // TILES_DEV
    return (slot_ids, slot_ids % TILES_DEV, device // N_BLK, device % N_BLK)


def draw_tile_rows(key, part):
    slot_ids, slot, group, member = slot_layout()
    spread = jax.random.randint(jax.random.fold_in(key, 21), slot_ids.shape, 0, GB, dtype=jnp.int32)
    skewed = spread * spread // GB
    return jnp.where(slot < RB_DEV, group * GB + member * RB_DEV + slot, group * GB + skewed)


def draw_tile_cols(key, part):
    slot_ids, slot, group, member = slot_layout()
    lowest = jnp.maximum(group * GB - REACH, 0)
    highest = jnp.minimum(group * GB + GB + REACH, NBLOCKS)
    raw_pick = jax.random.randint(jax.random.fold_in(key, 31), slot_ids.shape, 0, 1 << 20, dtype=jnp.int32)
    picked = lowest + raw_pick % (highest - lowest)
    picked = jnp.where(slot == RB_DEV, lowest, picked)
    picked = jnp.where(slot == RB_DEV + 1, highest - 1, picked)
    return jnp.where(slot < RB_DEV, group * GB + member * RB_DEV + slot, picked)


def draw_tile_count(key, part):
    device_count = N_ROWS * N_BLK
    spare = TILES_DEV - RB_DEV
    spread = jax.random.randint(jax.random.fold_in(key, 41), (device_count,), 0, spare + 1, dtype=jnp.int32)
    counts = TILES_DEV - spread * spread // spare
    first_pick = jax.random.randint(jax.random.fold_in(key, 42), (), 0, device_count, dtype=jnp.int32)
    offset_pick = jax.random.randint(jax.random.fold_in(key, 43), (), 0, device_count - 1, dtype=jnp.int32)
    second_pick = (first_pick + 1 + offset_pick) % device_count
    device_ids = jnp.arange(device_count, dtype=jnp.int32)
    counts = jnp.where(device_ids == first_pick, TILES_DEV, counts)
    counts = jnp.where(device_ids == second_pick, RB_DEV, counts)
    return counts.reshape(N_ROWS, N_BLK)


def setup_inputs(seed: int = 0) -> dict:
    key_of = jax.random.split(jax.random.key(seed), 6)
    start_block = draw_start_block(jax.random.fold_in(key_of[5], 71), 0)
    tile_vals = draw_tile_vals(jax.random.fold_in(key_of[5], 71), 0)
    tile_rows = draw_tile_rows(jax.random.fold_in(key_of[5], 71), 0)
    tile_cols = draw_tile_cols(jax.random.fold_in(key_of[5], 71), 0)
    tile_count = draw_tile_count(jax.random.fold_in(key_of[5], 71), 0)
    return {"start_block": start_block, "tile_vals": tile_vals, "tile_rows": tile_rows, "tile_cols": tile_cols, "tile_count": tile_count}


shift_term = -0.25
half_width = 0.75

def apply_operator(vectors, tile_sets, col_sets, row_sets, live_sets, inv_root):
    scaled = (vectors * inv_root[None, :]).reshape(K, NBLOCKS, TILE)

    def scan_step(total, scan_item):
        values, columns, rows_here, live_here = scan_item
        picked = jnp.take(scaled, columns, axis=1)
        products = jnp.einsum('ktb,tab->kta', picked, values * live_here[:, None, None], precision=lax.Precision.HIGHEST)
        return (total.at[:, rows_here, :].add(products), None)
    start_total = jnp.zeros((K, NBLOCKS, TILE), jnp.float32)
    total, _ = lax.scan(scan_step, start_total, (tile_sets, col_sets, row_sets, live_sets))
    applied = total.reshape(K, ROWS_ALL) * inv_root[None, :]
    return (shift_term * vectors - applied) / half_width

def reference(start_block, tile_vals, tile_rows, tile_cols, tile_count):
    device_count = N_ROWS * N_BLK
    tile_sets = tile_vals.reshape(device_count, TILES_DEV, TILE, TILE)
    row_sets = tile_rows.reshape(device_count, TILES_DEV)
    col_sets = tile_cols.reshape(device_count, TILES_DEV)
    slot_index = jnp.arange(TILES_DEV, dtype=jnp.int32)
    live_sets = (slot_index[None, :] < tile_count.reshape(device_count, 1)).astype(jnp.float32)
    row_sums = lax.optimization_barrier(jnp.sum(tile_sets, axis=3)) * live_sets[:, :, None]
    degree = jnp.zeros((NBLOCKS, TILE), jnp.float32).at[row_sets.reshape(-1)].add(row_sums.reshape(-1, TILE))
    inv_root = 1.0 / jnp.sqrt(degree.reshape(ROWS_ALL))
    previous = start_block
    current = apply_operator(start_block, tile_sets, col_sets, row_sets, live_sets, inv_root)
    for index in range(STEPS - 1):
        following = 2.0 * apply_operator(current, tile_sets, col_sets, row_sets, live_sets, inv_root) - previous
        previous = current
        current = following
    gram_sum = jnp.dot(current, current.T, precision=lax.Precision.HIGHEST) / ROWS_ALL
    factor = jnp.linalg.cholesky(gram_sum)
    return lax.linalg.triangular_solve(factor, current, left_side=True, lower=True)
```

```python
import functools

import jax
import jax.numpy as jnp
from jax import lax
from jax.experimental import pallas as pl
from jax.experimental.pallas import tpu as pltpu
from jax.sharding import PartitionSpec as P

STEPS = 3
CHAINS = 2
OUTER = 4
GROUP = 16
VMEM_BYTES = 40 << 20

shift_term = -0.25
half_width = 0.75


def split_bf16(x):
    high = x.astype(jnp.bfloat16)
    return high, (x - high.astype(jnp.float32)).astype(jnp.bfloat16)


def prepare_kernel(rows_ref, live_ref, vals_ref, cat_ref, degree_ref, *, tile):
    step = pl.program_id(0)

    @pl.when(step == 0)
    def _():
        degree_ref[...] = jnp.zeros_like(degree_ref)

    ones = jnp.ones((8, 2 * tile), jnp.bfloat16)
    for item in range(vals_ref.shape[0]):
        slot = step * vals_ref.shape[0] + item
        values = vals_ref[item] * (slot < live_ref[0]).astype(jnp.float32)
        high, low = split_bf16(values)
        cat_ref[item, :, :tile] = high
        cat_ref[item, :, tile:] = low
        sums = lax.dot_general(
            ones, cat_ref[item], (((1,), (1,)), ((), ())), preferred_element_type=jnp.float32
        )
        degree_ref[pl.ds(rows_ref[slot], 1), :] += sums[:1]


def prepare_tiles(tile_vals, row_local, live_count, group_blocks):
    slots, tile, _ = tile_vals.shape
    return pl.pallas_call(
        functools.partial(prepare_kernel, tile=tile),
        grid_spec=pltpu.PrefetchScalarGridSpec(
            num_scalar_prefetch=2,
            grid=(slots // GROUP,),
            in_specs=[pl.BlockSpec((GROUP, tile, tile), lambda i, *_: (i, 0, 0))],
            out_specs=[
                pl.BlockSpec((GROUP, tile, 2 * tile), lambda i, *_: (i, 0, 0)),
                pl.BlockSpec((group_blocks, tile), lambda i, *_: (0, 0)),
            ],
        ),
        out_shape=[
            jax.ShapeDtypeStruct((slots, tile, 2 * tile), jnp.bfloat16),
            jax.ShapeDtypeStruct((group_blocks, tile), jnp.float32),
        ],
        compiler_params=pltpu.CompilerParams(vmem_limit_bytes=VMEM_BYTES),
        name="prepare_tiles",
    )(row_local, live_count, tile_vals)


def store_split(cat_ref, slot, value):
    width, tile = value.shape
    high, low = split_bf16(value)
    cat_ref[slot, :width, :tile] = high
    cat_ref[slot, :width, tile:] = high
    cat_ref[slot, width:, :tile] = low
    cat_ref[slot, width:, tile:] = low


def product_kernel(cols_ref, rows_ref, place_ref, *refs, kind, inner, outer, own):
    refs = list(refs)
    pieces = [refs.pop(0) for _ in range(inner)]
    near, far = refs.pop(0), refs.pop(0)
    if kind == "first":
        inv_ref = refs.pop(0)
    else:
        last_ref = refs.pop(0)
        older_ref = refs.pop(0) if kind == "third" else None
    tiles_ref = refs.pop(0)
    state_ref = refs.pop(0)
    parts = [refs.pop(0) for _ in range(inner)]
    cat_ref, total_ref = refs
    step = pl.program_id(0)
    width, tile = state_ref.shape[1:]
    reach = inner * own

    @pl.when(step == 0)
    def _():
        total_ref[...] = jnp.zeros_like(total_ref)
        outer_index, inner_index, odd = place_ref[0], place_ref[1], place_ref[2]

        def advance(slot, value):
            if kind != "first":
                value = (2.0 / half_width) * (shift_term * last_ref[slot] - value)
                if kind == "third":
                    value = value - older_ref[slot]
                else:
                    value = 0.5 * value
            state_ref[slot] = value
            store_split(cat_ref, slot, value)

        for k in range(inner):
            block_inner = inner_index ^ k
            for z in range(outer):
                for j in range(own):
                    block = (z * inner + block_inner) * own + j
                    if kind == "first":
                        value = pieces[k][z ^ outer_index, j] * inv_ref[pl.ds(block, 1), :]
                    else:
                        value = pieces[k][z, j]
                    advance(reach + block, value)
            for j in range(own):
                offset = block_inner * own + j
                span = outer * reach + reach
                advance(jnp.where(odd == 1, 0, span) + offset, near[k, j])
                advance(jnp.where(odd == 1, span, 0) + offset, far[k, j])

    for item in range(tiles_ref.shape[0]):
        slot = step * tiles_ref.shape[0] + item
        both = lax.dot_general(
            cat_ref[cols_ref[slot]],
            tiles_ref[item],
            (((1,), (1,)), ((), ())),
            preferred_element_type=jnp.float32,
        )
        total_ref[rows_ref[slot]] += both[:width] + both[width:]

    @pl.when(step == pl.num_programs(0) - 1)
    def _():
        size = outer * own
        for k in range(inner):
            parts[k][...] = total_ref[k * size : (k + 1) * size].reshape(parts[k].shape)


def tile_products(kind, cols, rows, place, pieces, near, far, extra, tiles, inner):
    outer, own, width, tile = pieces[0].shape
    group_blocks = inner * outer * own
    window = group_blocks + 2 * inner * own
    slots = tiles.shape[0]
    whole = lambda shape: pl.BlockSpec(shape, lambda i, *_: (0,) * len(shape))
    operands = [*pieces, near, far, *extra]
    return pl.pallas_call(
        functools.partial(product_kernel, kind=kind, inner=inner, outer=outer, own=own),
        grid_spec=pltpu.PrefetchScalarGridSpec(
            num_scalar_prefetch=3,
            grid=(slots // GROUP,),
            in_specs=[whole(x.shape) for x in operands]
            + [pl.BlockSpec((GROUP, tile, 2 * tile), lambda i, *_: (i, 0, 0))],
            out_specs=[whole((window, width, tile))]
            + [whole((outer, own, width, tile))] * inner,
            scratch_shapes=[
                pltpu.VMEM((window, 2 * width, 2 * tile), jnp.bfloat16),
                pltpu.VMEM((group_blocks, width, tile), jnp.float32),
            ],
        ),
        out_shape=[jax.ShapeDtypeStruct((window, width, tile), jnp.float32)]
        + [jax.ShapeDtypeStruct((outer, own, width, tile), jnp.float32)] * inner,
        compiler_params=pltpu.CompilerParams(vmem_limit_bytes=VMEM_BYTES),
        name="products_" + kind,
    )(cols, rows, place, *operands, tiles)


def on_device(start_block, tile_vals, tile_rows, tile_cols, tile_count):
    vec_width, local_rows = start_block.shape
    tile = tile_vals.shape[1]
    own = local_rows // tile
    blk_count = lax.axis_size("blk")
    row_count = lax.axis_size("rows")
    outer = OUTER
    inner = blk_count // outer
    group_blocks = own * blk_count
    reach = group_blocks // outer
    rows_total = local_rows * blk_count * row_count
    group_index = lax.axis_index("rows")
    blk_index = lax.axis_index("blk")
    outer_index, inner_index = blk_index // inner, blk_index % inner
    odd = group_index % 2

    def over_inner(x, k):
        return lax.ppermute(
            x, "blk", [(z * inner + y, z * inner + (y ^ k)) for z in range(outer) for y in range(inner)]
        )

    def over_outer(x, k):
        return lax.ppermute(
            x, "blk", [(z * inner + y, (z ^ k) * inner + y) for z in range(outer) for y in range(inner)]
        )

    def over_rows(x, k):
        return lax.ppermute(x, "rows", [(i, i ^ k) for i in range(row_count)])

    def with_near(x):
        return lax.ppermute(x, "rows", [(i, i ^ 1) for i in range(row_count)])

    def with_far(x):
        pairs = [(i, i + 1) for i in range(1, row_count - 1, 2)]
        return lax.ppermute(x, "rows", pairs + [(b, a) for a, b in pairs])

    row_local = tile_rows - group_index * group_blocks
    col_local = tile_cols - (group_index * group_blocks - reach)
    place = jnp.stack([outer_index, inner_index, odd]).astype(jnp.int32)
    row_outer = row_local // reach
    row_inner = row_local // own % inner
    row_item = row_local % own
    rows_flat = ((row_inner ^ inner_index) * outer + row_outer) * own + row_item
    rows_last = ((row_inner ^ inner_index) * outer + (row_outer ^ outer_index)) * own + row_item

    tiles, degree = prepare_tiles(tile_vals, row_local, tile_count.reshape(1), group_blocks)

    blocks = start_block.reshape(vec_width, own, tile).transpose(1, 0, 2)
    chains = jnp.split(blocks, CHAINS, axis=1)
    gathered = []
    for chain in chains:
        stack = jnp.stack([chain] + [over_outer(chain, k) for k in range(1, outer)])
        gathered.append([stack] + [over_inner(stack, k) for k in range(1, inner)])

    bit = 1
    while bit < inner:
        degree = degree + over_inner(degree, bit)
        bit *= 2
    bit = 1
    while bit < outer:
        degree = degree + over_outer(degree, bit)
        bit *= 2
    inv_root = 1.0 / jnp.sqrt(degree)
    by_inner = (1.0 / degree).reshape(outer, inner, own, 1, tile)
    inv_own = lax.dynamic_index_in_dim(by_inner, inner_index, 1, keepdims=False)
    by_root = inv_root.reshape(outer, inner, own, 1, tile)

    def halo_pair(near_payload, far_payload):
        return with_near(near_payload), with_far(far_payload)

    near_outer = jnp.where(odd == 1, 0, outer - 1)
    far_outer = jnp.where(odd == 1, outer - 1, 0)

    def first_payload(pieces, which):
        rel = which ^ outer_index
        return jnp.stack(
            [
                lax.dynamic_index_in_dim(pieces[k], rel, 0, keepdims=False)
                * lax.dynamic_index_in_dim(
                    lax.dynamic_index_in_dim(by_root, which, 0, keepdims=False),
                    inner_index ^ k,
                    0,
                    keepdims=False,
                )
                for k in range(inner)
            ]
        )

    def later_payload(pieces, which):
        return jnp.stack([lax.dynamic_index_in_dim(p, which, 0, keepdims=False) for p in pieces])

    states = [[] for _ in range(CHAINS)]
    parts = [None] * CHAINS
    for c in range(CHAINS):
        near, far = halo_pair(
            first_payload(gathered[c], near_outer), first_payload(gathered[c], far_outer)
        )
        state, *parts[c] = tile_products(
            "first", col_local, rows_flat, place, gathered[c], near, far, [inv_root], tiles, inner
        )
        states[c].append(state)

    for index in range(1, STEPS):
        for c in range(CHAINS):
            total = parts[c][0]
            for k in range(1, inner):
                total = total + over_inner(parts[c][k], k)
            bit = 1
            while bit < outer:
                total = total + over_outer(total, bit)
                bit *= 2
            total = total * inv_own
            pieces = [total] + [over_inner(total, k) for k in range(1, inner)]
            near, far = halo_pair(
                later_payload(pieces, near_outer), later_payload(pieces, far_outer)
            )
            kind = "second" if index == 1 else "third"
            extra = [states[c][-1]] if index == 1 else [states[c][-1], states[c][-2]]
            rows = rows_last if index == STEPS - 1 else rows_flat
            state, *parts[c] = tile_products(
                kind, col_local, rows, place, pieces, near, far, extra, tiles, inner
            )
            states[c].append(state)

    own_degree = lax.dynamic_slice_in_dim(degree, blk_index * own, own, 0)[:, None, :]
    start = reach + blk_index * own
    filtered = []
    for c in range(CHAINS):
        total = parts[c][0]
        for k in range(1, inner):
            total = total + over_inner(parts[c][k], k)
        own_sum = total[0]
        for k in range(1, outer):
            own_sum = own_sum + over_outer(total[k], k)
        last = lax.dynamic_slice_in_dim(states[c][-1], start, own, 0)
        older = lax.dynamic_slice_in_dim(states[c][-2], start, own, 0)
        scaled = (2.0 / half_width) * (shift_term * last - own_sum / own_degree) - older
        filtered.append(scaled * jnp.sqrt(own_degree))
    current = jnp.concatenate(filtered, axis=1).transpose(1, 0, 2).reshape(vec_width, local_rows)

    gram_sum = jnp.dot(current, current.T, precision=lax.Precision.HIGHEST) / rows_total
    bit = 1
    while bit < row_count:
        gram_sum = gram_sum + over_rows(gram_sum, bit)
        bit *= 2
    bit = 1
    while bit < inner:
        gram_sum = gram_sum + over_inner(gram_sum, bit)
        bit *= 2
    bit = 1
    while bit < outer:
        gram_sum = gram_sum + over_outer(gram_sum, bit)
        bit *= 2
    factor = jnp.linalg.cholesky(gram_sum, symmetrize_input=False)
    return lax.linalg.triangular_solve(factor, current, left_side=True, lower=True)


def solution(mesh):
    in_specs = (
        P(None, ("rows", "blk")),
        P(("rows", "blk"), None, None),
        P(("rows", "blk")),
        P(("rows", "blk")),
        P("rows", "blk"),
    )
    out_specs = P(None, ("rows", "blk"))
    return jax.shard_map(
        on_device, mesh=mesh, in_specs=in_specs, out_specs=out_specs, check_vma=False
    )
```

```python
import functools

import jax
import jax.numpy as jnp
from jax import lax
from jax.experimental import pallas as pl
from jax.experimental.pallas import tpu as pltpu
from jax.sharding import PartitionSpec as P

STEPS = 3
CHAINS = 2
GROUP = 16
VMEM_BYTES = 40 << 20

shift_term = -0.25
half_width = 0.75


def split_bf16(x):
    high = x.astype(jnp.bfloat16)
    return high, (x - high.astype(jnp.float32)).astype(jnp.bfloat16)


def prepare_kernel(rows_ref, live_ref, vals_hbm, cat_hbm, degree_ref, vals_ref, cat_ref, in_sems, out_sems):
    slots, tile, _ = vals_ref.shape
    groups = [pl.ds(g * GROUP, GROUP) for g in range(slots // GROUP)]
    loads = [
        pltpu.make_async_copy(vals_hbm.at[g], vals_ref.at[g], in_sems.at[i])
        for i, g in enumerate(groups)
    ]
    stores = [
        pltpu.make_async_copy(cat_ref.at[g], cat_hbm.at[g], out_sems.at[i])
        for i, g in enumerate(groups)
    ]
    for load in loads:
        load.start()
    degree_ref[...] = jnp.zeros_like(degree_ref)
    ones = jnp.ones((8, 2 * tile), jnp.bfloat16)
    for slot in range(slots):
        if slot % GROUP == 0:
            loads[slot // GROUP].wait()
        values = vals_ref[slot] * (slot < live_ref[0]).astype(jnp.float32)
        high, low = split_bf16(values)
        cat_ref[slot, :, :tile] = high
        cat_ref[slot, :, tile:] = low
        sums = lax.dot_general(
            ones, cat_ref[slot], (((1,), (1,)), ((), ())), preferred_element_type=jnp.float32
        )
        degree_ref[pl.ds(rows_ref[slot], 1), :] += sums[:1]
        if slot % GROUP == GROUP - 1:
            stores[slot // GROUP].start()
    for store in stores:
        store.wait()


def prepare_tiles(tile_vals, row_local, live_count, group_blocks):
    slots, tile, _ = tile_vals.shape
    smem = pl.BlockSpec(memory_space=pltpu.SMEM)
    hbm = pl.BlockSpec(memory_space=pltpu.HBM)
    return pl.pallas_call(
        prepare_kernel,
        in_specs=[smem, smem, hbm],
        out_specs=[hbm, pl.BlockSpec(memory_space=pltpu.VMEM)],
        out_shape=[
            jax.ShapeDtypeStruct((slots, tile, 2 * tile), jnp.bfloat16),
            jax.ShapeDtypeStruct((group_blocks, tile), jnp.float32),
        ],
        scratch_shapes=[
            pltpu.VMEM(tile_vals.shape, jnp.float32),
            pltpu.VMEM((slots, tile, 2 * tile), jnp.bfloat16),
            pltpu.SemaphoreType.DMA((slots // GROUP,)),
            pltpu.SemaphoreType.DMA((slots // GROUP,)),
        ],
        compiler_params=pltpu.CompilerParams(vmem_limit_bytes=VMEM_BYTES),
        cost_estimate=pl.CostEstimate(
            flops=2_000_000_000, bytes_accessed=2 * tile_vals.size * 4, transcendentals=0
        ),
        name="prepare_tiles",
    )(row_local, live_count, tile_vals)


def store_split(cat_ref, slot, value):
    width, tile = value.shape
    high, low = split_bf16(value)
    cat_ref[slot, :width, :tile] = high
    cat_ref[slot, :width, tile:] = high
    cat_ref[slot, width:, :tile] = low
    cat_ref[slot, width:, tile:] = low


def product_kernel(cols_ref, rows_ref, place_ref, *refs, kind, pieces_count, outer_half):
    refs = list(refs)
    pieces = [refs.pop(0) for _ in range(pieces_count)]
    near, far = refs.pop(0), refs.pop(0)
    if kind == "first":
        inv_ref = refs.pop(0)
    else:
        last_ref = refs.pop(0)
        older_ref = refs.pop(0) if kind == "third" else None
    tiles_hbm, state_ref = refs.pop(0), refs.pop(0)
    parts = [refs.pop(0) for _ in range(pieces_count)]
    cat_ref, total_ref, tiles_ref, sems = refs
    width, tile = state_ref.shape[1:]
    reach = near.shape[0]
    part = total_ref.shape[0] // pieces_count
    slots = tiles_ref.shape[0]
    copies = [
        pltpu.make_async_copy(
            tiles_hbm.at[pl.ds(g * GROUP, GROUP)], tiles_ref.at[pl.ds(g * GROUP, GROUP)], sems.at[g]
        )
        for g in range(slots // GROUP)
    ]
    for copy in copies:
        copy.start()
    total_ref[...] = jnp.zeros_like(total_ref)
    quad, high, odd = place_ref[0], place_ref[1], place_ref[2]

    def advance(slot, value):
        if kind != "first":
            value = (2.0 / half_width) * (shift_term * last_ref[slot] - value)
            if kind == "third":
                value = value - older_ref[slot]
            else:
                value = 0.5 * value
        state_ref[slot] = value
        store_split(cat_ref, slot, value)

    for k in range(pieces_count):
        who = quad ^ k
        if kind == "first":
            own = part // outer_half
            for h in range(outer_half):
                block = ((h ^ high) * pieces_count + who) * own
                for j in range(own):
                    value = pieces[k][h * own + j] * inv_ref[pl.ds(block + j, 1), :]
                    advance(reach + block + j, value)
        else:
            for j in range(part):
                advance(reach + who * part + j, pieces[k][j])
    span = total_ref.shape[0] + reach
    for j in range(reach):
        advance(jnp.where(odd == 1, 0, span) + j, near[j])
        advance(jnp.where(odd == 1, span, 0) + j, far[j])

    for slot in range(slots):
        if slot % GROUP == 0:
            copies[slot // GROUP].wait()
        both = lax.dot_general(
            cat_ref[cols_ref[slot]],
            tiles_ref[slot],
            (((1,), (1,)), ((), ())),
            preferred_element_type=jnp.float32,
        )
        total_ref[rows_ref[slot]] += both[:width] + both[width:]

    for k in range(pieces_count):
        parts[k][...] = total_ref[k * part : (k + 1) * part]


def tile_products(kind, cols, rows, place, pieces, near, far, extra, tiles, outer_half):
    part, width, tile = pieces[0].shape
    count = len(pieces)
    group_blocks = count * part
    window = group_blocks + 2 * near.shape[0]
    slots = tiles.shape[0]
    vmem = pl.BlockSpec(memory_space=pltpu.VMEM)
    smem = pl.BlockSpec(memory_space=pltpu.SMEM)
    operands = [*pieces, near, far, *extra]
    return pl.pallas_call(
        functools.partial(
            product_kernel, kind=kind, pieces_count=count, outer_half=outer_half
        ),
        in_specs=[smem] * 3 + [vmem] * len(operands) + [pl.BlockSpec(memory_space=pltpu.HBM)],
        out_specs=[vmem] * (1 + count),
        scratch_shapes=[
            pltpu.VMEM((window, 2 * width, 2 * tile), jnp.bfloat16),
            pltpu.VMEM((group_blocks, width, tile), jnp.float32),
            pltpu.VMEM(tiles.shape, tiles.dtype),
            pltpu.SemaphoreType.DMA((slots // GROUP,)),
        ],
        out_shape=[jax.ShapeDtypeStruct((window, width, tile), jnp.float32)]
        + [jax.ShapeDtypeStruct((part, width, tile), jnp.float32)] * count,
        compiler_params=pltpu.CompilerParams(vmem_limit_bytes=VMEM_BYTES),
        cost_estimate=pl.CostEstimate(
            flops=3_000_000_000, bytes_accessed=slots * tile * tile * 4, transcendentals=0
        ),
        name="products_" + kind,
    )(cols, rows, place, *operands, tiles)


def on_device(start_block, tile_vals, tile_rows, tile_cols, tile_count):
    vec_width, local_rows = start_block.shape
    tile = tile_vals.shape[1]
    own = local_rows // tile
    blk_count = lax.axis_size("blk")
    row_count = lax.axis_size("rows")
    high_count = 2
    quad_count = blk_count // high_count
    group_blocks = own * blk_count
    part = group_blocks // quad_count
    reach = group_blocks // 4
    rows_total = local_rows * blk_count * row_count
    group_index = lax.axis_index("rows")
    blk_index = lax.axis_index("blk")
    high, quad = blk_index // quad_count, blk_index % quad_count
    odd = group_index % 2

    def over_blk(x, k):
        return lax.ppermute(x, "blk", [(i, i ^ k) for i in range(blk_count)])

    def over_rows(x, k):
        return lax.ppermute(x, "rows", [(i, i ^ k) for i in range(row_count)])

    def with_far(x):
        pairs = [(i, i + 1) for i in range(1, row_count - 1, 2)]
        return lax.ppermute(x, "rows", pairs + [(b, a) for a, b in pairs])

    def spread(x):
        return [x] + [over_blk(x, k) for k in range(1, quad_count)]

    def gather_sum(parts):
        total = parts[0]
        for k in range(1, quad_count):
            total = total + over_blk(parts[k], k)
        return total

    def all_sum(x):
        return x + over_blk(x, quad_count)

    row_local = tile_rows - group_index * group_blocks
    col_local = tile_cols - (group_index * group_blocks - reach)
    place = jnp.stack([quad, high, odd]).astype(jnp.int32)
    rows_flat = ((row_local // part) ^ quad) * part + row_local % part
    row_blk = row_local // own
    rows_last = ((row_blk % quad_count) ^ quad) * part
    rows_last = rows_last + ((row_blk // quad_count) ^ high) * own + row_local % own

    blocks = start_block.reshape(vec_width, own, tile).transpose(1, 0, 2)
    chains = jnp.split(blocks, CHAINS, axis=1)
    gathered = [
        spread(jnp.concatenate([chain, over_blk(chain, quad_count)])) for chain in chains
    ]

    tiles, degree = prepare_tiles(tile_vals, row_local, tile_count.reshape(1), group_blocks)
    degree = all_sum(sum(spread(degree)))
    inv_root = 1.0 / jnp.sqrt(degree)
    inv_part = lax.dynamic_slice_in_dim(1.0 / degree, quad * part, part, 0)[:, None, :]

    def select(pieces, which):
        value = pieces[0]
        for k in range(1, len(pieces)):
            value = jnp.where(which == k, pieces[k], value)
        return value

    def halos(block_of):
        near_base = jnp.where(odd == 1, 0, group_blocks - reach)
        far_base = jnp.where(odd == 1, group_blocks - reach, 0)
        return over_rows(block_of(near_base), 1), with_far(block_of(far_base))

    def first_blocks(pieces, base):
        found = []
        for m in range(reach // own):
            blk = base // own + m
            piece = select(pieces, (blk % quad_count) ^ quad)
            half = (blk // quad_count) ^ high
            found.append(jnp.where(half == 0, piece[:own], piece[own:]))
        root = lax.dynamic_slice_in_dim(inv_root, base, reach, 0)
        return jnp.concatenate(found) * root[:, None, :]

    def later_blocks(pieces, base):
        return jnp.concatenate(
            [select(pieces, (base // part + m) ^ quad) for m in range(reach // part)]
        )

    states = [[] for _ in range(CHAINS)]
    parts = [None] * CHAINS
    for c in range(CHAINS):
        near, far = halos(functools.partial(first_blocks, gathered[c]))
        state, *parts[c] = tile_products(
            "first", col_local, rows_flat, place, gathered[c], near, far, [inv_root], tiles, high_count
        )
        states[c].append(state)

    for index in range(1, STEPS):
        for c in range(CHAINS):
            total = all_sum(gather_sum(parts[c])) * inv_part
            pieces = spread(total)
            near, far = halos(functools.partial(later_blocks, pieces))
            kind = "second" if index == 1 else "third"
            extra = [states[c][-1]] if index == 1 else [states[c][-1], states[c][-2]]
            rows = rows_last if index == STEPS - 1 else rows_flat
            state, *parts[c] = tile_products(
                kind, col_local, rows, place, pieces, near, far, extra, tiles, high_count
            )
            states[c].append(state)

    own_degree = lax.dynamic_slice_in_dim(degree, blk_index * own, own, 0)[:, None, :]
    start = reach + blk_index * own
    filtered = []
    for c in range(CHAINS):
        total = gather_sum(parts[c])
        own_sum = total[:own] + over_blk(total[own:], quad_count)
        last = lax.dynamic_slice_in_dim(states[c][-1], start, own, 0)
        older = lax.dynamic_slice_in_dim(states[c][-2], start, own, 0)
        scaled = (2.0 / half_width) * (shift_term * last - own_sum / own_degree) - older
        filtered.append(scaled * jnp.sqrt(own_degree))
    current = jnp.concatenate(filtered, axis=1).transpose(1, 0, 2).reshape(vec_width, local_rows)

    gram_sum = jnp.dot(current, current.T, precision=lax.Precision.HIGHEST) / rows_total
    bit = 1
    while bit < row_count:
        gram_sum = gram_sum + over_rows(gram_sum, bit)
        bit *= 2
    gram_sum = all_sum(sum(spread(gram_sum)))
    factor = jnp.linalg.cholesky(gram_sum, symmetrize_input=False)
    return lax.linalg.triangular_solve(factor, current, left_side=True, lower=True)


def solution(mesh):
    in_specs = (
        P(None, ("rows", "blk")),
        P(("rows", "blk"), None, None),
        P(("rows", "blk")),
        P(("rows", "blk")),
        P("rows", "blk"),
    )
    out_specs = P(None, ("rows", "blk"))
    return jax.shard_map(
        on_device, mesh=mesh, in_specs=in_specs, out_specs=out_specs, check_vma=False
    )
```

```python
import functools

import jax
import jax.numpy as jnp
from jax import lax
from jax.experimental import pallas as pl
from jax.experimental.pallas import tpu as pltpu
from jax.sharding import PartitionSpec as P

STEPS = 3
CHAINS = 2
GROUP = 16
VMEM_BYTES = 16 << 20

shift_term = -0.25
half_width = 0.75


def split_bf16(x):
    high = x.astype(jnp.bfloat16)
    return high, (x - high.astype(jnp.float32)).astype(jnp.bfloat16)


def prepare_kernel(rows_ref, live_ref, vals_hbm, cat_ref, degree_ref, vals_ref, sems):
    slots, tile, _ = vals_ref.shape
    loads = [
        pltpu.make_async_copy(
            vals_hbm.at[pl.ds(g * GROUP, GROUP)], vals_ref.at[pl.ds(g * GROUP, GROUP)], sems.at[g]
        )
        for g in range(slots // GROUP)
    ]
    for load in loads:
        load.start()
    degree_ref[...] = jnp.zeros_like(degree_ref)
    ones = jnp.ones((8, 2 * tile), jnp.bfloat16)
    for slot in range(slots):
        if slot % GROUP == 0:
            loads[slot // GROUP].wait()
        values = vals_ref[slot] * (slot < live_ref[0]).astype(jnp.float32)
        high, low = split_bf16(values)
        cat_ref[slot, :, :tile] = high
        cat_ref[slot, :, tile:] = low
        sums = lax.dot_general(
            ones, cat_ref[slot], (((1,), (1,)), ((), ())), preferred_element_type=jnp.float32
        )
        degree_ref[pl.ds(rows_ref[slot], 1), :] += sums[:1]


def prepare_tiles(tile_vals, row_local, live_count, group_blocks):
    slots, tile, _ = tile_vals.shape
    smem = pl.BlockSpec(memory_space=pltpu.SMEM)
    vmem = pl.BlockSpec(memory_space=pltpu.VMEM)
    return pl.pallas_call(
        prepare_kernel,
        in_specs=[smem, smem, pl.BlockSpec(memory_space=pl.ANY)],
        out_specs=[vmem, vmem],
        out_shape=[
            pltpu.VMEM((slots, tile, 2 * tile), jnp.bfloat16),
            jax.ShapeDtypeStruct((group_blocks, tile), jnp.float32),
        ],
        scratch_shapes=[
            pltpu.VMEM(tile_vals.shape, jnp.float32),
            pltpu.SemaphoreType.DMA((slots // GROUP,)),
        ],
        compiler_params=pltpu.CompilerParams(vmem_limit_bytes=VMEM_BYTES),
        cost_estimate=pl.CostEstimate(
            flops=2_000_000_000, bytes_accessed=2 * tile_vals.size * 4, transcendentals=0
        ),
        name="prepare_tiles",
    )(row_local, live_count, pltpu.with_memory_space_constraint(tile_vals, pltpu.HBM))


def store_split(cat_ref, slot, value):
    width, tile = value.shape
    high, low = split_bf16(value)
    cat_ref[slot, :width, :tile] = high
    cat_ref[slot, :width, tile:] = high
    cat_ref[slot, width:, :tile] = low
    cat_ref[slot, width:, tile:] = low


def product_kernel(cols_ref, rows_ref, place_ref, *refs, kind, pieces_count, outer_half):
    refs = list(refs)
    pieces = [refs.pop(0) for _ in range(pieces_count)]
    near, far = refs.pop(0), refs.pop(0)
    if kind == "first":
        inv_ref = refs.pop(0)
    else:
        last_ref = refs.pop(0)
        older_ref = refs.pop(0) if kind == "third" else None
    tiles_ref, state_ref = refs.pop(0), refs.pop(0)
    parts = [refs.pop(0) for _ in range(pieces_count)]
    cat_ref, total_ref = refs
    width, tile = state_ref.shape[1:]
    reach = near.shape[0]
    part = total_ref.shape[0] // pieces_count
    slots = tiles_ref.shape[0]
    total_ref[...] = jnp.zeros_like(total_ref)
    quad, high, odd = place_ref[0], place_ref[1], place_ref[2]

    def advance(slot, value):
        if kind != "first":
            value = (2.0 / half_width) * (shift_term * last_ref[slot] - value)
            if kind == "third":
                value = value - older_ref[slot]
            else:
                value = 0.5 * value
        state_ref[slot] = value
        store_split(cat_ref, slot, value)

    for k in range(pieces_count):
        who = quad ^ k
        if kind == "first":
            own = part // outer_half
            for h in range(outer_half):
                block = ((h ^ high) * pieces_count + who) * own
                for j in range(own):
                    value = pieces[k][h * own + j] * inv_ref[pl.ds(block + j, 1), :]
                    advance(reach + block + j, value)
        else:
            for j in range(part):
                advance(reach + who * part + j, pieces[k][j])
    span = total_ref.shape[0] + reach
    for j in range(reach):
        advance(jnp.where(odd == 1, 0, span) + j, near[j])
        advance(jnp.where(odd == 1, span, 0) + j, far[j])

    for slot in range(slots):
        both = lax.dot_general(
            cat_ref[cols_ref[slot]],
            tiles_ref[slot],
            (((1,), (1,)), ((), ())),
            preferred_element_type=jnp.float32,
        )
        total_ref[rows_ref[slot]] += both[:width] + both[width:]

    for k in range(pieces_count):
        parts[k][...] = total_ref[k * part : (k + 1) * part]


def tile_products(kind, cols, rows, place, pieces, near, far, extra, tiles, outer_half):
    part, width, tile = pieces[0].shape
    count = len(pieces)
    group_blocks = count * part
    window = group_blocks + 2 * near.shape[0]
    slots = tiles.shape[0]
    vmem = pl.BlockSpec(memory_space=pltpu.VMEM)
    smem = pl.BlockSpec(memory_space=pltpu.SMEM)
    operands = [*pieces, near, far, *extra]
    return pl.pallas_call(
        functools.partial(
            product_kernel, kind=kind, pieces_count=count, outer_half=outer_half
        ),
        in_specs=[smem] * 3 + [vmem] * (len(operands) + 1),
        out_specs=[vmem] * (1 + count),
        scratch_shapes=[
            pltpu.VMEM((window, 2 * width, 2 * tile), jnp.bfloat16),
            pltpu.VMEM((group_blocks, width, tile), jnp.float32),
        ],
        out_shape=[jax.ShapeDtypeStruct((window, width, tile), jnp.float32)]
        + [jax.ShapeDtypeStruct((part, width, tile), jnp.float32)] * count,
        compiler_params=pltpu.CompilerParams(vmem_limit_bytes=VMEM_BYTES),
        cost_estimate=pl.CostEstimate(
            flops=3_000_000_000, bytes_accessed=slots * tile * tile * 4, transcendentals=0
        ),
        name="products_" + kind,
    )(cols, rows, place, *operands, pltpu.with_memory_space_constraint(tiles, pltpu.VMEM))


def gram_kernel(place_ref, *refs, chains, own):
    refs = list(refs)
    groups = [[refs.pop(0) for _ in range(4)] for _ in range(chains)]
    degree_ref, filtered_ref, gram_ref, all_ref = refs
    halves = groups[0][0].shape[0] // own
    width = groups[0][0].shape[1]
    for h in range(halves):
        for j in range(own):
            block = place_ref[h] + j
            degree = degree_ref[pl.ds(block, 1), :]
            for c, (mine, other, last, older) in enumerate(groups):
                total = mine[h * own + j] + other[(halves - 1 - h) * own + j]
                slot = place_ref[halves] + block
                value = (2.0 / half_width) * (shift_term * last[slot] - total / degree)
                value = (value - older[slot]) * jnp.sqrt(degree)
                all_ref[h * own + j, c * width : (c + 1) * width, :] = value
                if h == 0:
                    filtered_ref[j, c * width : (c + 1) * width, :] = value
    gram = jnp.zeros(gram_ref.shape, jnp.float32)
    for i in range(halves * own):
        block = all_ref[i]
        gram += lax.dot_general(
            block,
            block,
            (((1,), (1,)), ((), ())),
            precision=lax.Precision.HIGHEST,
            preferred_element_type=jnp.float32,
        )
    gram_ref[...] = gram


def gram_of(place, groups, degree, own):
    part, width, tile = groups[0][0].shape
    total = width * len(groups)
    smem = pl.BlockSpec(memory_space=pltpu.SMEM)
    vmem = pl.BlockSpec(memory_space=pltpu.VMEM)
    operands = [x for group in groups for x in group] + [degree]
    return pl.pallas_call(
        functools.partial(gram_kernel, chains=len(groups), own=own),
        in_specs=[smem] + [vmem] * len(operands),
        out_specs=[vmem, vmem],
        out_shape=[
            jax.ShapeDtypeStruct((own, total, tile), jnp.float32),
            jax.ShapeDtypeStruct((total, total), jnp.float32),
        ],
        scratch_shapes=[pltpu.VMEM((part, total, tile), jnp.float32)],
        compiler_params=pltpu.CompilerParams(vmem_limit_bytes=VMEM_BYTES),
        name="gram",
    )(place, *operands)


def solve_kernel(*refs, pieces, scale):
    parts, filtered_ref, out_ref, work_ref = refs[:pieces], *refs[pieces:]
    size = parts[0].shape[0]
    tile = filtered_ref.shape[2]
    gram = parts[0][...]
    for part in parts[1:]:
        gram = gram + part[...]
    row = lax.broadcasted_iota(jnp.int32, (size, size), 0)
    column = lax.broadcasted_iota(jnp.int32, (size, size), 1)
    work_ref[:, :size] = gram * scale
    work_ref[:, size:] = (row == column).astype(jnp.float32)
    step = 8
    wide = 2 * size
    count = size // step
    rows = [work_ref[step * i : step * (i + 1), :] for i in range(count)]
    sub = lax.broadcasted_iota(jnp.int32, (step, wide), 0)

    def spread_row(x, j):
        return jnp.broadcast_to(x[j : j + 1, :], (step, wide))

    for p in range(count):
        columns = {
            i: [
                jnp.broadcast_to(rows[i][:, step * p + j : step * p + j + 1], (step, wide))
                for j in range(step)
            ]
            for i in range(p, count)
        }
        for j in range(step):
            root = lax.rsqrt(spread_row(columns[p][j], j))
            pivot = spread_row(rows[p], j) * root
            heads = {k: spread_row(columns[p][k], j) * root for k in range(j + 1, step)}
            for i in range(p, count):
                factor = columns[i][j] * root
                if i == p:
                    factor = jnp.where(sub > j, factor, 0.0)
                rows[i] = rows[i] - factor * pivot
                for k in range(j + 1, step):
                    columns[i][k] = columns[i][k] - factor * heads[k]
            rows[p] = jnp.where(sub == j, pivot, rows[p])
        work_ref[step * p : step * (p + 1), :] = rows[p]
    inverse = work_ref[:, size:]
    for j in range(filtered_ref.shape[0]):
        out_ref[:, j * tile : (j + 1) * tile] = lax.dot_general(
            inverse,
            filtered_ref[j],
            (((1,), (0,)), ((), ())),
            precision=lax.Precision.HIGHEST,
            preferred_element_type=jnp.float32,
        )


def solve(parts, filtered, scale):
    own, total, tile = filtered.shape
    vmem = pl.BlockSpec(memory_space=pltpu.VMEM)
    return pl.pallas_call(
        functools.partial(solve_kernel, pieces=len(parts), scale=scale),
        in_specs=[vmem] * (len(parts) + 1),
        out_specs=vmem,
        out_shape=jax.ShapeDtypeStruct((total, own * tile), jnp.float32),
        scratch_shapes=[pltpu.VMEM((total, 2 * total), jnp.float32)],
        compiler_params=pltpu.CompilerParams(vmem_limit_bytes=VMEM_BYTES),
        name="solve",
    )(*parts, filtered)


def on_device(start_block, tile_vals, tile_rows, tile_cols, tile_count):
    vec_width, local_rows = start_block.shape
    tile = tile_vals.shape[1]
    own = local_rows // tile
    blk_count = lax.axis_size("blk")
    row_count = lax.axis_size("rows")
    high_count = 2
    quad_count = blk_count // high_count
    group_blocks = own * blk_count
    part = group_blocks // quad_count
    reach = group_blocks // 4
    rows_total = local_rows * blk_count * row_count
    group_index = lax.axis_index("rows")
    blk_index = lax.axis_index("blk")
    high, quad = blk_index // quad_count, blk_index % quad_count
    odd = group_index % 2

    def over_blk(x, k):
        return lax.ppermute(x, "blk", [(i, i ^ k) for i in range(blk_count)])

    def over_rows(x, k):
        return lax.ppermute(x, "rows", [(i, i ^ k) for i in range(row_count)])

    def with_far(x):
        pairs = [(i, i + 1) for i in range(1, row_count - 1, 2)]
        return lax.ppermute(x, "rows", pairs + [(b, a) for a, b in pairs])

    def spread(x):
        return [x] + [over_blk(x, k) for k in range(1, quad_count)]

    def gather_sum(parts):
        total = parts[0]
        for k in range(1, quad_count):
            total = total + over_blk(parts[k], k)
        return total

    def after(x, y):
        return lax.optimization_barrier((x, y))[0]

    def all_sum(x):
        return x + over_blk(x, quad_count)

    row_local = tile_rows - group_index * group_blocks
    col_local = tile_cols - (group_index * group_blocks - reach)
    place = jnp.stack([quad, high, odd]).astype(jnp.int32)
    rows_flat = ((row_local // part) ^ quad) * part + row_local % part
    row_blk = row_local // own
    rows_last = ((row_blk % quad_count) ^ quad) * part
    rows_last = rows_last + ((row_blk // quad_count) ^ high) * own + row_local % own

    blocks = start_block.reshape(vec_width, own, tile).transpose(1, 0, 2)
    chains = jnp.split(blocks, CHAINS, axis=1)
    others = [over_blk(chain, quad_count) for chain in chains]
    gathered = [spread(jnp.concatenate(pair)) for pair in zip(chains, others)]
    tile_vals = after(tile_vals, others[0])

    tiles, degree = prepare_tiles(tile_vals, row_local, tile_count.reshape(1), group_blocks)
    degree = all_sum(sum(spread(degree)))
    inv_root = 1.0 / jnp.sqrt(degree)
    inv_part = lax.dynamic_slice_in_dim(1.0 / degree, quad * part, part, 0)[:, None, :]

    def select(pieces, which):
        value = pieces[0]
        for k in range(1, len(pieces)):
            value = jnp.where(which == k, pieces[k], value)
        return value

    def halos(block_of):
        near_base = jnp.where(odd == 1, 0, group_blocks - reach)
        far_base = jnp.where(odd == 1, group_blocks - reach, 0)
        return over_rows(block_of(near_base), 1), with_far(block_of(far_base))

    def first_blocks(pieces, base):
        found = []
        for m in range(reach // own):
            blk = base // own + m
            piece = select(pieces, (blk % quad_count) ^ quad)
            half = (blk // quad_count) ^ high
            found.append(jnp.where(half == 0, piece[:own], piece[own:]))
        root = lax.dynamic_slice_in_dim(inv_root, base, reach, 0)
        return jnp.concatenate(found) * root[:, None, :]

    def later_blocks(pieces, base):
        return jnp.concatenate(
            [select(pieces, (base // part + m) ^ quad) for m in range(reach // part)]
        )

    states = [[] for _ in range(CHAINS)]
    parts = [None] * CHAINS
    for c in range(CHAINS):
        near, far = halos(functools.partial(first_blocks, gathered[c]))
        state, *parts[c] = tile_products(
            "first", col_local, rows_flat, place, gathered[c], near, far, [inv_root], tiles, high_count
        )
        states[c].append(state)

    for index in range(1, STEPS):
        kind = "second" if index == 1 else "third"
        rows = rows_last if index == STEPS - 1 else rows_flat
        first_sums = [gather_sum(parts[c]) for c in range(CHAINS)]
        for c in range(CHAINS - 1):
            first_sums[c] = after(first_sums[c], parts[c + 1][0])
        totals = [all_sum(x) * inv_part for x in first_sums]
        for c in range(CHAINS - 1):
            totals[c] = after(totals[c], first_sums[c + 1])
        pieces = []
        for c in range(CHAINS):
            if c:
                totals[c] = after(totals[c], pieces[c - 1][1])
            pieces.append(spread(totals[c]))
        for c in range(CHAINS):
            mine = pieces[c] if c == CHAINS - 1 else after(pieces[c], totals[c + 1])
            near, far = halos(functools.partial(later_blocks, mine))
            if c < CHAINS - 1:
                near = after(near, pieces[c + 1][1:])
            state, *parts[c] = tile_products(
                kind, col_local, rows, place, mine, near, far,
                [states[c][-1 - i] for i in range(index)], tiles, high_count,
            )
            states[c].append(state)

    last_sums = [gather_sum(parts[c]) for c in range(CHAINS)]
    groups = [
        [last_sums[c], over_blk(last_sums[c], quad_count), states[c][-1], states[c][-2]]
        for c in range(CHAINS)
    ]
    offsets = [((h ^ high) * quad_count + quad) * own for h in range(high_count)]
    gram_place = jnp.stack([*offsets, jnp.full((), reach, offsets[0].dtype)]).astype(jnp.int32)
    filtered, gram = gram_of(gram_place, groups, degree, own)

    def over_all(x, rows_bit, blk_bit):
        pairs = [
            (i * row_count + j, (i ^ blk_bit) * row_count + (j ^ rows_bit))
            for i in range(blk_count)
            for j in range(row_count)
        ]
        return lax.ppermute(x, ("blk", "rows"), pairs)

    bits = [(1 << i, 0) for i in range(1, row_count.bit_length() - 1)]
    bits += [(0, 1 << i) for i in range(quad_count.bit_length() - 1)]
    stages = [[(1, 0)]]
    while bits:
        first, *second = bits[:2]
        bits = bits[2:]
        stages.append([first] + [x for y in second for x in (y, (first[0] ^ y[0], first[1] ^ y[1]))])
    pieces = [gram]
    for stage in stages:
        gram = sum(pieces[1:], pieces[0])
        pieces = [gram] + [over_all(gram, *bit) for bit in stage]
    return solve(pieces, filtered, 1.0 / rows_total)


def solution(mesh):
    in_specs = (
        P(None, ("rows", "blk")),
        P(("rows", "blk"), None, None),
        P(("rows", "blk")),
        P(("rows", "blk")),
        P("rows", "blk"),
    )
    out_specs = P(None, ("rows", "blk"))
    return jax.shard_map(
        on_device, mesh=mesh, in_specs=in_specs, out_specs=out_specs, check_vma=False
    )
```

```python
import functools

import jax
import jax.numpy as jnp
from jax import lax
from jax.experimental import pallas as pl
from jax.experimental.pallas import tpu as pltpu
from jax.sharding import PartitionSpec as P

STEPS = 3
CHAINS = 2
HALVES = 2
GROUP = 16
VMEM_BYTES = 16 << 20

shift_term = -0.25
half_width = 0.75

VMEM = pl.BlockSpec(memory_space=pltpu.VMEM)
SMEM = pl.BlockSpec(memory_space=pltpu.SMEM)
FULL = lax.Precision.HIGHEST


def call(kernel, out_shape, operands, in_specs=None, out_specs=None, scratch=(), flops=0, nbytes=0):
    many = isinstance(out_shape, list)
    return pl.pallas_call(
        kernel,
        in_specs=in_specs or [VMEM] * len(operands),
        out_specs=out_specs or ([VMEM] * len(out_shape) if many else VMEM),
        out_shape=out_shape,
        scratch_shapes=list(scratch),
        compiler_params=pltpu.CompilerParams(vmem_limit_bytes=VMEM_BYTES),
        cost_estimate=pl.CostEstimate(flops=flops, bytes_accessed=nbytes, transcendentals=0),
        name=kernel.func.__name__ if isinstance(kernel, functools.partial) else kernel.__name__,
    )(*operands)


def floats(*shape):
    return jax.ShapeDtypeStruct(shape, jnp.float32)


def split_bf16(x):
    high = x.astype(jnp.bfloat16)
    return high, (x - high.astype(jnp.float32)).astype(jnp.bfloat16)


def contract(a, b, dims, precision=None):
    return lax.dot_general(
        a, b, (dims, ((), ())), precision=precision, preferred_element_type=jnp.float32
    )


def prepare(table_ref, vals_hbm, cat_ref, degree_ref, vals_ref, sems):
    slots, tile, _ = vals_ref.shape
    loads = [
        pltpu.make_async_copy(
            vals_hbm.at[pl.ds(g * GROUP, GROUP)], vals_ref.at[pl.ds(g * GROUP, GROUP)], sems.at[g]
        )
        for g in range(slots // GROUP)
    ]
    for load in loads:
        load.start()
    degree_ref[...] = jnp.zeros_like(degree_ref)
    ones = jnp.ones((8, 2 * tile), jnp.bfloat16)
    live = table_ref[2 * slots]
    for slot in range(slots):
        if slot % GROUP == 0:
            loads[slot // GROUP].wait()
        values = vals_ref[slot] * (slot < live).astype(jnp.float32)
        high, low = split_bf16(values)
        cat_ref[slot, :, :tile] = high
        cat_ref[slot, :, tile:] = low
        sums = contract(ones, cat_ref[slot], ((1,), (1,)))
        degree_ref[pl.ds(table_ref[slots + slot], 1), :] += sums[:1]


def prepare_tiles(tile_vals, table, group_blocks):
    slots, tile, _ = tile_vals.shape
    return call(
        prepare,
        [pltpu.VMEM((slots, tile, 2 * tile), jnp.bfloat16), floats(group_blocks, tile)],
        [table, pltpu.with_memory_space_constraint(tile_vals, pltpu.HBM)],
        in_specs=[SMEM, pl.BlockSpec(memory_space=pl.ANY)],
        scratch=[
            pltpu.VMEM(tile_vals.shape, jnp.float32),
            pltpu.SemaphoreType.DMA((slots // GROUP,)),
        ],
        flops=2_000_000_000,
        nbytes=2 * tile_vals.size * 4,
    )


def join(flags_ref, chain_ref, other_ref, *refs):
    out_ref = refs[-1]
    own = chain_ref.shape[0]
    low = flags_ref[1, :1, :] == 0
    for j in range(own):
        mine, other = chain_ref[j], other_ref[j]
        out_ref[j] = jnp.where(low, mine, other)
        out_ref[own + j] = jnp.where(low, other, mine)
    if len(refs) == 2:
        out_ref[2 * own :] = refs[0][...].reshape(out_ref[2 * own :].shape)


def join_halves(flags, chain, other, degree=None):
    own, width, tile = chain.shape
    extra = 0 if degree is None else degree.shape[0] // width
    operands = [flags, chain, other] + ([] if degree is None else [degree])
    return call(join, floats(2 * own + extra, width, tile), operands)


def add_degrees(*refs, part):
    sources, out_ref = refs[:-1], refs[-1]
    tile = out_ref.shape[1]
    count = out_ref.shape[0] // part
    whole = [
        ref[ref.shape[0] - out_ref.shape[0] * tile // (ref.shape[1] * tile) :].reshape(-1, tile)
        for ref in sources
    ]
    for m in range(count):
        total = whole[0][m * part : (m + 1) * part]
        for k in range(1, len(whole)):
            total = total + whole[k][(m ^ k) * part : ((m ^ k) + 1) * part]
        out_ref[m * part : (m + 1) * part, :] = total


def roots(mine_ref, other_ref, root_ref, degree_ref, inverse_ref):
    degree = mine_ref[...] + other_ref[...]
    root_ref[...] = 1.0 / jnp.sqrt(degree)
    part = degree_ref.shape[0]
    degree_ref[...] = degree[:part]
    inverse_ref[...] = 1.0 / degree[:part]


def add(*refs, scaled):
    refs = list(refs)
    out_ref = refs.pop()
    scale_ref = refs.pop() if scaled else None
    for j in range(out_ref.shape[0]):
        total = refs[0][j]
        for ref in refs[1:]:
            total = total + ref[j]
        out_ref[j] = total * scale_ref[j : j + 1, :] if scaled else total


def add_all(arrays, scale=None):
    return call(
        functools.partial(add, scaled=scale is not None),
        floats(*arrays[0].shape),
        list(arrays) + ([] if scale is None else [scale]),
    )


def halo(flags_ref, *refs, own, rooted):
    refs = list(refs)
    far_ref, near_ref = refs.pop(), refs.pop()
    root_ref = refs.pop() if rooted else None
    count = len(refs)
    part = HALVES * own
    quad, odd = flags_ref[0, :1, :], flags_ref[2, :1, :] == 1
    for m in range(near_ref.shape[0] // own):
        low, high = m, count - near_ref.shape[0] // own + m
        for j in range(own):

            def block(k, h):
                value = refs[k][h * own + j]
                if rooted:
                    at = k * part + h * own + j
                    value = value * root_ref[at : at + 1, :]
                return value

            bottom, top = block(0, 0), block(0, HALVES - 1)
            for k in range(1, count):
                bottom = jnp.where((quad ^ k) == low, block(k, 0), bottom)
                top = jnp.where((quad ^ k) == high, block(k, HALVES - 1), top)
            near_ref[m * own + j] = jnp.where(odd, bottom, top)
            far_ref[m * own + j] = jnp.where(odd, top, bottom)


def halo_payloads(flags, pieces, own, reach, root=None):
    _, width, tile = pieces[0].shape
    operands = [flags, *pieces] + ([] if root is None else [root])
    return call(
        functools.partial(halo, own=own, rooted=root is not None),
        [floats(reach, width, tile)] * 2,
        operands,
    )


def products(table_ref, *refs, count, kind):
    refs = list(refs)
    pieces = [refs.pop(0) for _ in range(count)]
    near, far = refs.pop(0), refs.pop(0)
    if kind == "first":
        root_ref = refs.pop(0)
    else:
        last_ref = refs.pop(0)
        older_ref = refs.pop(0) if kind == "third" else None
    tiles_ref, state_ref = refs.pop(0), refs.pop(0)
    parts = [refs.pop(0) for _ in range(count)]
    cat_ref, total_ref = refs
    _, width, tile = state_ref.shape
    reach = near.shape[0]
    part = total_ref.shape[0] // count
    slots = tiles_ref.shape[0]
    total_ref[...] = jnp.zeros_like(total_ref)

    def advance(slot, value):
        if kind != "first":
            value = (2.0 / half_width) * (shift_term * last_ref[slot] - value)
            if kind == "third":
                value = value - older_ref[slot]
            else:
                value = 0.5 * value
        state_ref[slot] = value
        high, low = split_bf16(value)
        cat_ref[slot, :width, :tile] = high
        cat_ref[slot, :width, tile:] = high
        cat_ref[slot, width:, :tile] = low
        cat_ref[slot, width:, tile:] = low

    for k in range(count):
        for j in range(part):
            slot = k * part + j
            value = pieces[k][j]
            if kind == "first":
                value = value * root_ref[slot : slot + 1, :]
            advance(slot, value)
    for j in range(reach):
        advance(count * part + j, near[j])
        advance(count * part + reach + j, far[j])

    for slot in range(slots):
        both = contract(cat_ref[table_ref[slot]], tiles_ref[slot], ((1,), (1,)))
        total_ref[table_ref[slots + slot]] += both[:width] + both[width:]

    for k in range(count):
        parts[k][...] = total_ref[k * part : (k + 1) * part]


def tile_products(kind, table, pieces, near, far, extra, tiles, group_blocks):
    reach, width, tile = near.shape
    count = len(pieces)
    window = group_blocks + 2 * reach
    operands = [table, *pieces, near, far, *extra]
    operands.append(pltpu.with_memory_space_constraint(tiles, pltpu.VMEM))
    return call(
        functools.partial(products, kind=kind, count=count),
        [floats(window, width, tile)] + [floats(group_blocks // count, width, tile)] * count,
        operands,
        in_specs=[SMEM] + [VMEM] * (len(operands) - 1),
        scratch=[
            pltpu.VMEM((window, 2 * width, 2 * tile), jnp.bfloat16),
            pltpu.VMEM((group_blocks, width, tile), jnp.float32),
        ],
        flops=3_000_000_000,
        nbytes=tiles.size * 2,
    )


def gram(flags_ref, degree_ref, *refs, own):
    refs = list(refs)
    all_ref, gram_ref, filtered_ref = refs.pop(), refs.pop(), refs.pop()
    groups = [refs[i : i + 4] for i in range(0, len(refs), 4)]
    width = groups[0][0].shape[1]
    low = flags_ref[1, :1, :] == 0
    total = jnp.zeros(gram_ref.shape, jnp.float32)
    for i in range(HALVES * own):
        degree = degree_ref[i : i + 1, :]
        root, inverse = jnp.sqrt(degree), 1.0 / degree
        for c, (mine, other, last, older) in enumerate(groups):
            value = (mine[i] + other[i]) * inverse
            value = (2.0 / half_width) * (shift_term * last[i] - value) - older[i]
            all_ref[i, c * width : (c + 1) * width, :] = value * root
        block = all_ref[i]
        total += contract(block, block, ((1,), (1,)), FULL)
    for j in range(own):
        filtered_ref[j] = jnp.where(low, all_ref[j], all_ref[own + j])
    gram_ref[...] = total


def gram_of(flags, degree, groups, own):
    part, width, tile = groups[0][0].shape
    total = width * len(groups)
    return call(
        functools.partial(gram, own=own),
        [floats(own, total, tile), floats(total, total)],
        [flags, degree] + [x for group in groups for x in group],
        scratch=[pltpu.VMEM((part, total, tile), jnp.float32)],
    )


def solve(*refs, scale):
    parts, (filtered_ref, out_ref, work_ref) = refs[:-3], refs[-3:]
    size = parts[0].shape[0]
    tile = filtered_ref.shape[2]
    total = parts[0][...]
    for piece in parts[1:]:
        total = total + piece[...]
    row = lax.broadcasted_iota(jnp.int32, (size, size), 0)
    column = lax.broadcasted_iota(jnp.int32, (size, size), 1)
    work_ref[:, :size] = total * scale
    work_ref[:, size:] = (row == column).astype(jnp.float32)
    step = 8
    wide = 2 * size
    count = size // step
    rows = [work_ref[step * i : step * (i + 1), :] for i in range(count)]
    sub = lax.broadcasted_iota(jnp.int32, (step, wide), 0)

    def spread_row(x, j):
        return jnp.broadcast_to(x[j : j + 1, :], (step, wide))

    for p in range(count):
        columns = {
            i: [
                jnp.broadcast_to(rows[i][:, step * p + j : step * p + j + 1], (step, wide))
                for j in range(step)
            ]
            for i in range(p, count)
        }
        for j in range(step):
            root = lax.rsqrt(spread_row(columns[p][j], j))
            pivot = spread_row(rows[p], j) * root
            heads = {k: spread_row(columns[p][k], j) * root for k in range(j + 1, step)}
            for i in range(p, count):
                factor = columns[i][j] * root
                if i == p:
                    factor = jnp.where(sub > j, factor, 0.0)
                rows[i] = rows[i] - factor * pivot
                for k in range(j + 1, step):
                    columns[i][k] = columns[i][k] - factor * heads[k]
            rows[p] = jnp.where(sub == j, pivot, rows[p])
        work_ref[step * p : step * (p + 1), :] = rows[p]
    inverse = work_ref[:, size:]
    for j in range(filtered_ref.shape[0]):
        out_ref[:, j * tile : (j + 1) * tile] = contract(
            inverse, filtered_ref[j], ((1,), (0,)), FULL
        )


def solve_of(parts, filtered, scale):
    own, total, tile = filtered.shape
    return call(
        functools.partial(solve, scale=scale),
        floats(total, own * tile),
        [*parts, filtered],
        scratch=[pltpu.VMEM((total, 2 * total), jnp.float32)],
    )


def after(x, y):
    return lax.optimization_barrier((x, y))[0]


def on_device(start_block, tile_vals, tile_rows, tile_cols, tile_count):
    vec_width, local_rows = start_block.shape
    tile = tile_vals.shape[1]
    own = local_rows // tile
    blk_count = lax.axis_size("blk")
    row_count = lax.axis_size("rows")
    quad_count = blk_count // HALVES
    group_blocks = own * blk_count
    part = HALVES * own
    reach = group_blocks // 4
    rows_total = local_rows * blk_count * row_count
    width = vec_width // CHAINS
    group_index = lax.axis_index("rows")
    blk_index = lax.axis_index("blk")
    high, quad, odd = blk_index // quad_count, blk_index & (quad_count - 1), group_index & 1

    def over_blk(x, k):
        return lax.ppermute(x, "blk", [(i, i ^ k) for i in range(blk_count)])

    def over_rows(x, k):
        return lax.ppermute(x, "rows", [(i, i ^ k) for i in range(row_count)])

    def over_all(x, rows_bit, blk_bit):
        pairs = [
            (i * row_count + j, (i ^ blk_bit) * row_count + (j ^ rows_bit))
            for i in range(blk_count)
            for j in range(row_count)
        ]
        return lax.ppermute(x, ("blk", "rows"), pairs)

    def with_far(x):
        pairs = [(i, i + 1) for i in range(1, row_count - 1, 2)]
        return lax.ppermute(x, "rows", pairs + [(b, a) for a, b in pairs])

    def spread(x):
        return [x] + [over_blk(x, k) for k in range(1, quad_count)]

    def gather_sum(parts):
        return add_all([parts[0]] + [over_blk(parts[k], k) for k in range(1, quad_count)])

    def place(block):
        blk = block // own
        return ((blk & (quad_count - 1)) ^ quad) * part + (blk // quad_count) * own + block % own

    shift = group_index * group_blocks
    cols, rows = tile_cols - shift, tile_rows - shift
    left = group_blocks + jnp.where(odd == 1, 0, reach) + reach + cols
    right = group_blocks + jnp.where(odd == 1, reach, 0) + cols - group_blocks
    cols = jnp.where(cols < 0, left, jnp.where(cols < group_blocks, place(cols), right))
    table = jnp.concatenate([cols, place(rows), tile_count.reshape(1)])
    flags = jnp.stack([quad, high, odd]).astype(jnp.int32)
    flags = jnp.broadcast_to(flags[:, None, None], (3, 8, tile))
    blocks = start_block.reshape(vec_width, own, tile).transpose(1, 0, 2)
    chains = jnp.split(blocks, CHAINS, axis=1)
    tile_vals, table, flags, chains = lax.optimization_barrier((tile_vals, table, flags, chains))

    tiles, degree = prepare_tiles(tile_vals, table, group_blocks)
    others = [over_blk(chain, quad_count) for chain in chains]
    others[0] = after(others[0], others[1:])
    gathered = [spread(join_halves(flags, chains[0], others[0], degree))]
    for chain, other in zip(chains[1:], others[1:]):
        gathered.append(spread(join_halves(flags, chain, other)))
    degree = call(
        functools.partial(add_degrees, part=part), floats(group_blocks, tile), gathered[0]
    )
    other = after(over_blk(degree, quad_count), [x[1] for x in gathered[1:]])
    root, own_degree, inverse = call(
        roots,
        [floats(group_blocks, tile), floats(part, tile), floats(part, tile)],
        [degree, other],
    )

    states = [[] for _ in range(CHAINS)]
    parts = [None] * CHAINS
    for c in range(CHAINS):
        near, far = halo_payloads(flags, gathered[c], own, reach, root)
        near, far = over_rows(near, 1), with_far(far)
        if c + 1 < CHAINS:
            gathered[c + 1] = gathered[c + 1][:2] + after(gathered[c + 1][2:], near)
        state, *parts[c] = tile_products(
            "first", table, gathered[c], near, far, [root], tiles, group_blocks
        )
        states[c].append(state)

    for index in range(1, STEPS):
        kind = "second" if index == 1 else "third"
        sums = [gather_sum(parts[c]) for c in range(CHAINS)]
        for c in range(CHAINS - 1):
            sums[c] = after(sums[c], parts[c + 1][0])
        totals, pieces = [], []
        for c in range(CHAINS):
            mine = after(sums[c], other) if c else sums[c]
            other = over_blk(mine, quad_count)
            arrived = after(other, pieces[c - 1][1]) if c else other
            totals.append(add_all([mine, arrived], inverse))
            pieces.append(spread(totals[c]))
        for c in range(CHAINS):
            mine = after(pieces[c], totals[c + 1]) if c + 1 < CHAINS else pieces[c]
            near, far = halo_payloads(flags, mine, own, reach)
            near, far = over_rows(near, 1), with_far(far)
            if c + 1 < CHAINS:
                near = after(near, pieces[c + 1][1:])
            state, *parts[c] = tile_products(
                kind, table, mine, near, far,
                [states[c][-1 - i] for i in range(index)], tiles, group_blocks,
            )
            states[c].append(state)

    sums = [gather_sum(parts[c]) for c in range(CHAINS)]
    for c in range(CHAINS - 1):
        sums[c] = after(sums[c], parts[c + 1][0])
    groups = [
        [sums[c], over_blk(sums[c], quad_count), states[c][-1], states[c][-2]]
        for c in range(CHAINS)
    ]
    filtered, total = gram_of(flags, own_degree, groups, own)

    bits = [(1 << i, 0) for i in range(1, row_count.bit_length() - 1)]
    bits += [(0, 1 << i) for i in range(quad_count.bit_length() - 1)]
    stages = [[(1, 0)]]
    while bits:
        first, *second = bits[:2]
        bits = bits[2:]
        stages.append([first] + [x for y in second for x in (y, (first[0] ^ y[0], first[1] ^ y[1]))])
    pieces = [total]
    for stage in stages:
        total = sum(pieces[1:], pieces[0])
        pieces = [total] + [over_all(total, *bit) for bit in stage]
    return solve_of(pieces, filtered, 1.0 / rows_total)


def solution(mesh):
    in_specs = (
        P(None, ("rows", "blk")),
        P(("rows", "blk"), None, None),
        P(("rows", "blk")),
        P(("rows", "blk")),
        P("rows", "blk"),
    )
    out_specs = P(None, ("rows", "blk"))
    return jax.shard_map(
        on_device, mesh=mesh, in_specs=in_specs, out_specs=out_specs, check_vma=False
    )
```

```python
import functools

import jax
import jax.numpy as jnp
from jax import lax
from jax.experimental import pallas as pl
from jax.experimental.pallas import tpu as pltpu
from jax.sharding import PartitionSpec as P

STEPS = 3
CHAINS = 2
HALVES = 2
GROUP = 16
VMEM_BYTES = 16 << 20

shift_term = -0.25
half_width = 0.75

VMEM = pl.BlockSpec(memory_space=pltpu.VMEM)
SMEM = pl.BlockSpec(memory_space=pltpu.SMEM)
FULL = lax.Precision.HIGHEST


def call(kernel, out_shape, operands, in_specs=None, out_specs=None, scratch=(), flops=0, nbytes=0):
    many = isinstance(out_shape, list)
    return pl.pallas_call(
        kernel,
        in_specs=in_specs or [VMEM] * len(operands),
        out_specs=out_specs or ([VMEM] * len(out_shape) if many else VMEM),
        out_shape=out_shape,
        scratch_shapes=list(scratch),
        compiler_params=pltpu.CompilerParams(vmem_limit_bytes=VMEM_BYTES),
        cost_estimate=pl.CostEstimate(flops=flops, bytes_accessed=nbytes, transcendentals=0),
        name=kernel.func.__name__ if isinstance(kernel, functools.partial) else kernel.__name__,
    )(*operands)


def floats(*shape):
    return jax.ShapeDtypeStruct(shape, jnp.float32)


def split_bf16(x):
    high = x.astype(jnp.bfloat16)
    return high, (x - high.astype(jnp.float32)).astype(jnp.bfloat16)


def contract(a, b, dims, precision=None):
    return lax.dot_general(
        a, b, (dims, ((), ())), precision=precision, preferred_element_type=jnp.float32
    )


def prepare(table_ref, vals_hbm, cat_ref, degree_ref, vals_ref, sems):
    slots, tile, _ = vals_ref.shape
    loads = [
        pltpu.make_async_copy(
            vals_hbm.at[pl.ds(g * GROUP, GROUP)], vals_ref.at[pl.ds(g * GROUP, GROUP)], sems.at[g]
        )
        for g in range(slots // GROUP)
    ]
    for load in loads:
        load.start()
    degree_ref[...] = jnp.zeros_like(degree_ref)
    ones = jnp.ones((8, 2 * tile), jnp.bfloat16)
    live = table_ref[2 * slots]
    for slot in range(slots):
        if slot % GROUP == 0:
            loads[slot // GROUP].wait()
        values = vals_ref[slot] * (slot < live).astype(jnp.float32)
        high, low = split_bf16(values)
        cat_ref[slot, :, :tile] = high
        cat_ref[slot, :, tile:] = low
        sums = contract(ones, cat_ref[slot], ((1,), (1,)))
        degree_ref[pl.ds(table_ref[slots + slot], 1), :] += sums[:1]


def prepare_tiles(tile_vals, table, group_blocks):
    slots, tile, _ = tile_vals.shape
    return call(
        prepare,
        [pltpu.VMEM((slots, tile, 2 * tile), jnp.bfloat16), floats(group_blocks, tile)],
        [table, pltpu.with_memory_space_constraint(tile_vals, pltpu.HBM)],
        in_specs=[SMEM, pl.BlockSpec(memory_space=pl.ANY)],
        scratch=[
            pltpu.VMEM(tile_vals.shape, jnp.float32),
            pltpu.SemaphoreType.DMA((slots // GROUP,)),
        ],
        flops=2_000_000_000,
        nbytes=2 * tile_vals.size * 4,
    )


def join(flags_ref, chain_ref, other_ref, *refs):
    out_ref = refs[-1]
    own = chain_ref.shape[0]
    low = flags_ref[1, :1, :] == 0
    for j in range(own):
        mine, other = chain_ref[j], other_ref[j]
        out_ref[j] = jnp.where(low, mine, other)
        out_ref[own + j] = jnp.where(low, other, mine)
    if len(refs) == 2:
        out_ref[2 * own :] = refs[0][...].reshape(out_ref[2 * own :].shape)


def join_halves(flags, chain, other, degree=None):
    own, width, tile = chain.shape
    extra = 0 if degree is None else degree.shape[0] // width
    operands = [flags, chain, other] + ([] if degree is None else [degree])
    return call(join, floats(2 * own + extra, width, tile), operands)


def roots(*refs, part):
    sources, (root_ref, degree_ref, inverse_ref) = refs[:-3], refs[-3:]
    for m in range(root_ref.shape[0] // part):
        total = sources[0][m * part : (m + 1) * part, :]
        for k in range(1, len(sources)):
            total = total + sources[k][(m ^ k) * part : ((m ^ k) + 1) * part, :]
        root_ref[m * part : (m + 1) * part, :] = 1.0 / jnp.sqrt(total)
        if m == 0:
            degree_ref[...] = total
            inverse_ref[...] = 1.0 / total


def add(*refs, scaled):
    refs = list(refs)
    out_ref = refs.pop()
    scale_ref = refs.pop() if scaled else None
    for j in range(out_ref.shape[0]):
        total = refs[0][j]
        for ref in refs[1:]:
            total = total + ref[j]
        out_ref[j] = total * scale_ref[j : j + 1, :] if scaled else total


def add_all(arrays, scale=None):
    return call(
        functools.partial(add, scaled=scale is not None),
        floats(*arrays[0].shape),
        list(arrays) + ([] if scale is None else [scale]),
    )


def halo(flags_ref, *refs, own, rooted):
    refs = list(refs)
    far_ref, near_ref = refs.pop(), refs.pop()
    root_ref = refs.pop() if rooted else None
    count = len(refs)
    part = HALVES * own
    quad, odd = flags_ref[0, :1, :], flags_ref[2, :1, :] == 1
    for m in range(near_ref.shape[0] // own):
        low, high = m, count - near_ref.shape[0] // own + m
        for j in range(own):

            def block(k, h):
                value = refs[k][h * own + j]
                if rooted:
                    at = k * part + h * own + j
                    value = value * root_ref[at : at + 1, :]
                return value

            bottom, top = block(0, 0), block(0, HALVES - 1)
            for k in range(1, count):
                bottom = jnp.where((quad ^ k) == low, block(k, 0), bottom)
                top = jnp.where((quad ^ k) == high, block(k, HALVES - 1), top)
            near_ref[m * own + j] = jnp.where(odd, bottom, top)
            far_ref[m * own + j] = jnp.where(odd, top, bottom)


def halo_payloads(flags, pieces, own, reach, root=None):
    _, width, tile = pieces[0].shape
    operands = [flags, *pieces] + ([] if root is None else [root])
    return call(
        functools.partial(halo, own=own, rooted=root is not None),
        [floats(reach, width, tile)] * 2,
        operands,
    )


def products(table_hbm, *refs, count, kind):
    refs = list(refs)
    sem = refs.pop()
    table_ref = refs.pop()
    fetch = pltpu.make_async_copy(table_hbm, table_ref, sem)
    fetch.start()
    pieces = [refs.pop(0) for _ in range(count)]
    near, far = refs.pop(0), refs.pop(0)
    if kind == "first":
        root_ref = refs.pop(0)
    else:
        last_ref = refs.pop(0)
        older_ref = refs.pop(0) if kind == "third" else None
    tiles_ref, state_ref = refs.pop(0), refs.pop(0)
    parts = [refs.pop(0) for _ in range(count)]
    cat_ref, total_ref = refs
    _, width, tile = state_ref.shape
    reach = near.shape[0]
    part = total_ref.shape[0] // count
    slots = tiles_ref.shape[0]
    total_ref[...] = jnp.zeros_like(total_ref)

    def advance(slot, value):
        if kind != "first":
            value = (2.0 / half_width) * (shift_term * last_ref[slot] - value)
            if kind == "third":
                value = value - older_ref[slot]
            else:
                value = 0.5 * value
        state_ref[slot] = value
        high, low = split_bf16(value)
        cat_ref[slot, :width, :tile] = high
        cat_ref[slot, :width, tile:] = high
        cat_ref[slot, width:, :tile] = low
        cat_ref[slot, width:, tile:] = low

    for k in range(count):
        for j in range(part):
            slot = k * part + j
            value = pieces[k][j]
            if kind == "first":
                value = value * root_ref[slot : slot + 1, :]
            advance(slot, value)
    for j in range(reach):
        advance(count * part + j, near[j])
        advance(count * part + reach + j, far[j])

    fetch.wait()
    for slot in range(slots):
        both = contract(cat_ref[table_ref[slot]], tiles_ref[slot], ((1,), (1,)))
        total_ref[table_ref[slots + slot]] += both[:width] + both[width:]

    for k in range(count):
        parts[k][...] = total_ref[k * part : (k + 1) * part]


def tile_products(kind, table, pieces, near, far, extra, tiles, group_blocks):
    reach, width, tile = near.shape
    count = len(pieces)
    window = group_blocks + 2 * reach
    operands = [table, *pieces, near, far, *extra]
    operands.append(pltpu.with_memory_space_constraint(tiles, pltpu.VMEM))
    return call(
        functools.partial(products, kind=kind, count=count),
        [floats(window, width, tile)] + [floats(group_blocks // count, width, tile)] * count,
        operands,
        in_specs=[pl.BlockSpec(memory_space=pl.ANY)] + [VMEM] * (len(operands) - 1),
        scratch=[
            pltpu.VMEM((window, 2 * width, 2 * tile), jnp.bfloat16),
            pltpu.VMEM((group_blocks, width, tile), jnp.float32),
            pltpu.SMEM(table.shape, table.dtype),
            pltpu.SemaphoreType.DMA(()),
        ],
        flops=3_000_000_000,
        nbytes=tiles.size * 2,
    )


def gram(flags_ref, degree_ref, *refs, own):
    refs = list(refs)
    all_ref, gram_ref, filtered_ref = refs.pop(), refs.pop(), refs.pop()
    groups = [refs[i : i + 4] for i in range(0, len(refs), 4)]
    width = groups[0][0].shape[1]
    low = flags_ref[1, :1, :] == 0
    total = jnp.zeros(gram_ref.shape, jnp.float32)
    for i in range(HALVES * own):
        degree = degree_ref[i : i + 1, :]
        root, inverse = jnp.sqrt(degree), 1.0 / degree
        for c, (mine, other, last, older) in enumerate(groups):
            value = (mine[i] + other[i]) * inverse
            value = (2.0 / half_width) * (shift_term * last[i] - value) - older[i]
            all_ref[i, c * width : (c + 1) * width, :] = value * root
        block = all_ref[i]
        total += contract(block, block, ((1,), (1,)), FULL)
    for j in range(own):
        filtered_ref[j] = jnp.where(low, all_ref[j], all_ref[own + j])
    gram_ref[...] = total


def gram_of(flags, degree, groups, own):
    part, width, tile = groups[0][0].shape
    total = width * len(groups)
    return call(
        functools.partial(gram, own=own),
        [floats(own, total, tile), floats(total, total)],
        [flags, degree] + [x for group in groups for x in group],
        scratch=[pltpu.VMEM((part, total, tile), jnp.float32)],
    )


def solve(*refs, scale):
    parts, (filtered_ref, out_ref, work_ref) = refs[:-3], refs[-3:]
    size = parts[0].shape[0]
    tile = filtered_ref.shape[2]
    total = parts[0][...]
    for piece in parts[1:]:
        total = total + piece[...]
    row = lax.broadcasted_iota(jnp.int32, (size, size), 0)
    column = lax.broadcasted_iota(jnp.int32, (size, size), 1)
    work_ref[:, :size] = total * scale
    work_ref[:, size:] = (row == column).astype(jnp.float32)
    step = 8
    wide = 2 * size
    count = size // step
    rows = [work_ref[step * i : step * (i + 1), :] for i in range(count)]
    sub = lax.broadcasted_iota(jnp.int32, (step, wide), 0)

    def spread_row(x, j):
        return jnp.broadcast_to(x[j : j + 1, :], (step, wide))

    for p in range(count):
        columns = {
            i: [
                jnp.broadcast_to(rows[i][:, step * p + j : step * p + j + 1], (step, wide))
                for j in range(step)
            ]
            for i in range(p, count)
        }
        for j in range(step):
            root = lax.rsqrt(spread_row(columns[p][j], j))
            pivot = spread_row(rows[p], j) * root
            heads = {k: spread_row(columns[p][k], j) * root for k in range(j + 1, step)}
            for i in range(p, count):
                factor = columns[i][j] * root
                if i == p:
                    factor = jnp.where(sub > j, factor, 0.0)
                rows[i] = rows[i] - factor * pivot
                for k in range(j + 1, step):
                    columns[i][k] = columns[i][k] - factor * heads[k]
            rows[p] = jnp.where(sub == j, pivot, rows[p])
        work_ref[step * p : step * (p + 1), :] = rows[p]
    inverse = work_ref[:, size:]
    for j in range(filtered_ref.shape[0]):
        out_ref[:, j * tile : (j + 1) * tile] = contract(
            inverse, filtered_ref[j], ((1,), (0,)), FULL
        )


def solve_of(parts, filtered, scale):
    own, total, tile = filtered.shape
    return call(
        functools.partial(solve, scale=scale),
        floats(total, own * tile),
        [*parts, filtered],
        scratch=[pltpu.VMEM((total, 2 * total), jnp.float32)],
    )


def after(x, y):
    return lax.optimization_barrier((x, y))[0]


def on_device(start_block, tile_vals, tile_rows, tile_cols, tile_count):
    vec_width, local_rows = start_block.shape
    tile = tile_vals.shape[1]
    own = local_rows // tile
    blk_count = lax.axis_size("blk")
    row_count = lax.axis_size("rows")
    quad_count = blk_count // HALVES
    group_blocks = own * blk_count
    part = HALVES * own
    reach = group_blocks // 4
    rows_total = local_rows * blk_count * row_count
    width = vec_width // CHAINS
    group_index = lax.axis_index("rows")
    blk_index = lax.axis_index("blk")
    high, quad, odd = blk_index // quad_count, blk_index & (quad_count - 1), group_index & 1

    def over_blk(x, k):
        return lax.ppermute(x, "blk", [(i, i ^ k) for i in range(blk_count)])

    def over_rows(x, k):
        return lax.ppermute(x, "rows", [(i, i ^ k) for i in range(row_count)])

    def over_all(x, rows_bit, blk_bit):
        pairs = [
            (i * row_count + j, (i ^ blk_bit) * row_count + (j ^ rows_bit))
            for i in range(blk_count)
            for j in range(row_count)
        ]
        return lax.ppermute(x, ("blk", "rows"), pairs)

    def with_far(x):
        pairs = [(i, i + 1) for i in range(1, row_count - 1, 2)]
        return lax.ppermute(x, "rows", pairs + [(b, a) for a, b in pairs])

    def spread(x):
        return [x] + [over_blk(x, k) for k in range(1, quad_count)]

    def gather_sum(parts):
        return add_all([parts[0]] + [over_blk(parts[k], k) for k in range(1, quad_count)])

    def place(block):
        blk = block // own
        return ((blk & (quad_count - 1)) ^ quad) * part + (blk // quad_count) * own + block % own

    shift = group_index * group_blocks
    cols, rows = tile_cols - shift, tile_rows - shift
    left = group_blocks + jnp.where(odd == 1, 0, reach) + reach + cols
    right = group_blocks + jnp.where(odd == 1, reach, 0) + cols - group_blocks
    cols = jnp.where(cols < 0, left, jnp.where(cols < group_blocks, place(cols), right))
    table = jnp.concatenate([cols, place(rows), tile_count.reshape(1)])
    flags = jnp.stack([quad, high, odd]).astype(jnp.int32)
    flags = jnp.broadcast_to(flags[:, None, None], (3, 8, tile))
    blocks = start_block.reshape(vec_width, own, tile).transpose(1, 0, 2)
    chains = jnp.split(blocks, CHAINS, axis=1)
    tile_vals, table, flags = lax.optimization_barrier((tile_vals, table, flags))

    tiles, degree = prepare_tiles(tile_vals, table, group_blocks)
    others = [over_blk(chain, quad_count) for chain in chains]
    others[0] = after(others[0], [degree, *others[1:]])
    other = over_blk(degree, quad_count)
    gathered = [spread(join_halves(flags, x, y)) for x, y in zip(chains, others)]
    other = after(other, [x[1] for x in gathered])
    degrees = spread(add_all([degree[None], other[None]])[0])
    root, own_degree, inverse = call(
        functools.partial(roots, part=part),
        [floats(group_blocks, tile), floats(part, tile), floats(part, tile)],
        degrees,
    )

    states = [[] for _ in range(CHAINS)]
    parts = [None] * CHAINS
    for c in range(CHAINS):
        near, far = halo_payloads(flags, gathered[c], own, reach, root)
        near, far = over_rows(near, 1), with_far(far)
        if c + 1 < CHAINS:
            gathered[c + 1] = gathered[c + 1][:2] + after(gathered[c + 1][2:], near)
        state, *parts[c] = tile_products(
            "first", table, gathered[c], near, far, [root], tiles, group_blocks
        )
        states[c].append(state)

    for index in range(1, STEPS):
        kind = "second" if index == 1 else "third"
        sums = [gather_sum(parts[c]) for c in range(CHAINS)]
        for c in range(CHAINS - 1):
            sums[c] = after(sums[c], parts[c + 1][0])
        totals, pieces = [], []
        for c in range(CHAINS):
            mine = after(sums[c], other) if c else sums[c]
            other = over_blk(mine, quad_count)
            arrived = after(other, pieces[c - 1][1]) if c else other
            totals.append(add_all([mine, arrived], inverse))
            pieces.append(spread(totals[c]))
        for c in range(CHAINS):
            mine = after(pieces[c], totals[c + 1]) if c + 1 < CHAINS else pieces[c]
            near, far = halo_payloads(flags, mine, own, reach)
            near, far = over_rows(near, 1), with_far(far)
            if c + 1 < CHAINS:
                near = after(near, pieces[c + 1][1:])
            state, *parts[c] = tile_products(
                kind, table, mine, near, far,
                [states[c][-1 - i] for i in range(index)], tiles, group_blocks,
            )
            states[c].append(state)

    sums = [gather_sum(parts[c]) for c in range(CHAINS)]
    for c in range(CHAINS - 1):
        sums[c] = after(sums[c], parts[c + 1][0])
    groups = [
        [sums[c], over_blk(sums[c], quad_count), states[c][-1], states[c][-2]]
        for c in range(CHAINS)
    ]
    filtered, total = gram_of(flags, own_degree, groups, own)

    bits = [(1 << i, 0) for i in range(row_count.bit_length() - 1)]
    bits += [(0, 1 << i) for i in range(quad_count.bit_length() - 1)]
    stages = []
    while bits:
        first, *second = bits[:2]
        bits = bits[2:]
        stages.append([first] + [x for y in second for x in (y, (first[0] ^ y[0], first[1] ^ y[1]))])
    pieces = [total]
    for stage in stages:
        total = sum(pieces[1:], pieces[0])
        pieces = [total] + [over_all(total, *bit) for bit in stage]
    return solve_of(pieces, filtered, 1.0 / rows_total)


def solution(mesh):
    in_specs = (
        P(None, ("rows", "blk")),
        P(("rows", "blk"), None, None),
        P(("rows", "blk")),
        P(("rows", "blk")),
        P("rows", "blk"),
    )
    out_specs = P(None, ("rows", "blk"))
    return jax.shard_map(
        on_device, mesh=mesh, in_specs=in_specs, out_specs=out_specs, check_vma=False
    )
```

```python
import functools

import jax
import jax.numpy as jnp
from jax import lax
from jax.experimental import pallas as pl
from jax.experimental.pallas import tpu as pltpu
from jax.sharding import PartitionSpec as P

STEPS = 3
CHAINS = 2
HALVES = 2
GROUP = 16
VMEM_BYTES = 16 << 20

shift_term = -0.25
half_width = 0.75

VMEM = pl.BlockSpec(memory_space=pltpu.VMEM)
SMEM = pl.BlockSpec(memory_space=pltpu.SMEM)
FULL = lax.Precision.HIGHEST


def call(kernel, out_shape, operands, in_specs=None, out_specs=None, scratch=(), flops=0, nbytes=0):
    many = isinstance(out_shape, list)
    return pl.pallas_call(
        kernel,
        in_specs=in_specs or [VMEM] * len(operands),
        out_specs=out_specs or ([VMEM] * len(out_shape) if many else VMEM),
        out_shape=out_shape,
        scratch_shapes=list(scratch),
        compiler_params=pltpu.CompilerParams(vmem_limit_bytes=VMEM_BYTES),
        cost_estimate=pl.CostEstimate(flops=flops, bytes_accessed=nbytes, transcendentals=0),
        name=kernel.func.__name__ if isinstance(kernel, functools.partial) else kernel.__name__,
    )(*operands)


def floats(*shape):
    return jax.ShapeDtypeStruct(shape, jnp.float32)


def split_bf16(x):
    high = x.astype(jnp.bfloat16)
    return high, (x - high.astype(jnp.float32)).astype(jnp.bfloat16)


def contract(a, b, dims, precision=None):
    return lax.dot_general(
        a, b, (dims, ((), ())), precision=precision, preferred_element_type=jnp.float32
    )


def prepare(table_ref, vals_hbm, cat_ref, degree_ref, vals_ref, sems):
    slots, tile, _ = vals_ref.shape
    loads = [
        pltpu.make_async_copy(
            vals_hbm.at[pl.ds(g * GROUP, GROUP)], vals_ref.at[pl.ds(g * GROUP, GROUP)], sems.at[g]
        )
        for g in range(slots // GROUP)
    ]
    for load in loads:
        load.start()
    degree_ref[...] = jnp.zeros_like(degree_ref)
    ones = jnp.ones((8, 2 * tile), jnp.bfloat16)
    live = table_ref[2 * slots]
    for slot in range(slots):
        if slot % GROUP == 0:
            loads[slot // GROUP].wait()
        values = vals_ref[slot] * (slot < live).astype(jnp.float32)
        high, low = split_bf16(values)
        cat_ref[slot, :, :tile] = high
        cat_ref[slot, :, tile:] = low
        sums = contract(ones, cat_ref[slot], ((1,), (1,)))
        degree_ref[pl.ds(table_ref[slots + slot], 1), :] += sums[:1]


def prepare_tiles(tile_vals, table, group_blocks):
    slots, tile, _ = tile_vals.shape
    return call(
        prepare,
        [pltpu.VMEM((slots, tile, 2 * tile), jnp.bfloat16), floats(group_blocks, tile)],
        [table, pltpu.with_memory_space_constraint(tile_vals, pltpu.HBM)],
        in_specs=[SMEM, pl.BlockSpec(memory_space=pl.ANY)],
        scratch=[
            pltpu.VMEM(tile_vals.shape, jnp.float32),
            pltpu.SemaphoreType.DMA((slots // GROUP,)),
        ],
        flops=2_000_000_000,
        nbytes=2 * tile_vals.size * 4,
    )


def join(flags_ref, chain_ref, other_ref, *refs):
    out_ref = refs[-1]
    own = chain_ref.shape[0]
    low = flags_ref[1, :1, :] == 0
    for j in range(own):
        mine, other = chain_ref[j], other_ref[j]
        out_ref[j] = jnp.where(low, mine, other)
        out_ref[own + j] = jnp.where(low, other, mine)
    if len(refs) == 2:
        out_ref[2 * own :] = refs[0][...].reshape(out_ref[2 * own :].shape)


def join_halves(flags, chain, other, degree=None):
    own, width, tile = chain.shape
    extra = 0 if degree is None else degree.shape[0] // width
    operands = [flags, chain, other] + ([] if degree is None else [degree])
    return call(join, floats(2 * own + extra, width, tile), operands)


def roots(*refs, part):
    sources, (root_ref, degree_ref, inverse_ref) = refs[:-3], refs[-3:]
    for m in range(root_ref.shape[0] // part):
        total = sources[0][m * part : (m + 1) * part, :]
        for k in range(1, len(sources)):
            total = total + sources[k][(m ^ k) * part : ((m ^ k) + 1) * part, :]
        root_ref[m * part : (m + 1) * part, :] = 1.0 / jnp.sqrt(total)
        if m == 0:
            degree_ref[...] = total
            inverse_ref[...] = 1.0 / total


def add(*refs, scaled):
    refs = list(refs)
    out_ref = refs.pop()
    scale_ref = refs.pop() if scaled else None
    for j in range(out_ref.shape[0]):
        total = refs[0][j]
        for ref in refs[1:]:
            total = total + ref[j]
        out_ref[j] = total * scale_ref[j : j + 1, :] if scaled else total


def add_all(arrays, scale=None):
    return call(
        functools.partial(add, scaled=scale is not None),
        floats(*arrays[0].shape),
        list(arrays) + ([] if scale is None else [scale]),
    )


def halo(flags_ref, *refs, own, rooted):
    refs = list(refs)
    far_ref, near_ref = refs.pop(), refs.pop()
    root_ref = refs.pop() if rooted else None
    count = len(refs)
    part = HALVES * own
    quad, odd = flags_ref[0, :1, :], flags_ref[2, :1, :] == 1
    for m in range(near_ref.shape[0] // own):
        low, high = m, count - near_ref.shape[0] // own + m
        for j in range(own):

            def block(k, h):
                value = refs[k][h * own + j]
                if rooted:
                    at = k * part + h * own + j
                    value = value * root_ref[at : at + 1, :]
                return value

            bottom, top = block(0, 0), block(0, HALVES - 1)
            for k in range(1, count):
                bottom = jnp.where((quad ^ k) == low, block(k, 0), bottom)
                top = jnp.where((quad ^ k) == high, block(k, HALVES - 1), top)
            near_ref[m * own + j] = jnp.where(odd, bottom, top)
            far_ref[m * own + j] = jnp.where(odd, top, bottom)


def halo_payloads(flags, pieces, own, reach, root=None):
    _, width, tile = pieces[0].shape
    operands = [flags, *pieces] + ([] if root is None else [root])
    return call(
        functools.partial(halo, own=own, rooted=root is not None),
        [floats(reach, width, tile)] * 2,
        operands,
    )


def products(table_hbm, *refs, count, kind):
    refs = list(refs)
    sem = refs.pop()
    table_ref = refs.pop()
    fetch = pltpu.make_async_copy(table_hbm, table_ref, sem)
    fetch.start()
    pieces = [refs.pop(0) for _ in range(count)]
    near, far = refs.pop(0), refs.pop(0)
    if kind == "first":
        root_ref = refs.pop(0)
    else:
        last_ref = refs.pop(0)
        older_ref = refs.pop(0) if kind == "third" else None
    tiles_ref, state_ref = refs.pop(0), refs.pop(0)
    parts = [refs.pop(0) for _ in range(count)]
    cat_ref, total_ref = refs
    _, width, tile = state_ref.shape
    reach = near.shape[0]
    part = total_ref.shape[0] // count
    slots = tiles_ref.shape[0]
    total_ref[...] = jnp.zeros_like(total_ref)

    def advance(slot, value):
        if kind != "first":
            value = (2.0 / half_width) * (shift_term * last_ref[slot] - value)
            if kind == "third":
                value = value - older_ref[slot]
            else:
                value = 0.5 * value
        state_ref[slot] = value
        high, low = split_bf16(value)
        cat_ref[slot, :width, :tile] = high
        cat_ref[slot, :width, tile:] = high
        cat_ref[slot, width:, :tile] = low
        cat_ref[slot, width:, tile:] = low

    for k in range(count):
        for j in range(part):
            slot = k * part + j
            value = pieces[k][j]
            if kind == "first":
                value = value * root_ref[slot : slot + 1, :]
            advance(slot, value)
    for j in range(reach):
        advance(count * part + j, near[j])
        advance(count * part + reach + j, far[j])

    fetch.wait()
    for slot in range(slots):
        both = contract(cat_ref[table_ref[slot]], tiles_ref[slot], ((1,), (1,)))
        total_ref[table_ref[slots + slot]] += both[:width] + both[width:]

    for k in range(count):
        parts[k][...] = total_ref[k * part : (k + 1) * part]


def tile_products(kind, table, pieces, near, far, extra, tiles, group_blocks):
    reach, width, tile = near.shape
    count = len(pieces)
    window = group_blocks + 2 * reach
    operands = [table, *pieces, near, far, *extra]
    operands.append(pltpu.with_memory_space_constraint(tiles, pltpu.VMEM))
    return call(
        functools.partial(products, kind=kind, count=count),
        [floats(window, width, tile)] + [floats(group_blocks // count, width, tile)] * count,
        operands,
        in_specs=[pl.BlockSpec(memory_space=pl.ANY)] + [VMEM] * (len(operands) - 1),
        scratch=[
            pltpu.VMEM((window, 2 * width, 2 * tile), jnp.bfloat16),
            pltpu.VMEM((group_blocks, width, tile), jnp.float32),
            pltpu.SMEM(table.shape, table.dtype),
            pltpu.SemaphoreType.DMA(()),
        ],
        flops=3_000_000_000,
        nbytes=tiles.size * 2,
    )


def gram(flags_ref, degree_ref, *refs, own):
    refs = list(refs)
    all_ref, gram_ref, filtered_ref = refs.pop(), refs.pop(), refs.pop()
    groups = [refs[i : i + 4] for i in range(0, len(refs), 4)]
    width = groups[0][0].shape[1]
    low = flags_ref[1, :1, :] == 0
    total = jnp.zeros(gram_ref.shape, jnp.float32)
    for i in range(HALVES * own):
        degree = degree_ref[i : i + 1, :]
        root, inverse = jnp.sqrt(degree), 1.0 / degree
        for c, (mine, other, last, older) in enumerate(groups):
            value = (mine[i] + other[i]) * inverse
            value = (2.0 / half_width) * (shift_term * last[i] - value) - older[i]
            all_ref[i, c * width : (c + 1) * width, :] = value * root
        block = all_ref[i]
        total += contract(block, block, ((1,), (1,)), FULL)
    for j in range(own):
        filtered_ref[j] = jnp.where(low, all_ref[j], all_ref[own + j])
    gram_ref[...] = total


def gram_of(flags, degree, groups, own):
    part, width, tile = groups[0][0].shape
    total = width * len(groups)
    return call(
        functools.partial(gram, own=own),
        [floats(own, total, tile), floats(total, total)],
        [flags, degree] + [x for group in groups for x in group],
        scratch=[pltpu.VMEM((part, total, tile), jnp.float32)],
    )


def solve(*refs, scale):
    parts, (filtered_ref, out_ref, work_ref) = refs[:-3], refs[-3:]
    size = parts[0].shape[0]
    tile = filtered_ref.shape[2]
    total = parts[0][...]
    for piece in parts[1:]:
        total = total + piece[...]
    row = lax.broadcasted_iota(jnp.int32, (size, size), 0)
    column = lax.broadcasted_iota(jnp.int32, (size, size), 1)
    work_ref[:, :size] = total * scale
    work_ref[:, size:] = (row == column).astype(jnp.float32)
    step = 8
    wide = 2 * size
    count = size // step
    rows = [work_ref[step * i : step * (i + 1), :] for i in range(count)]
    sub = lax.broadcasted_iota(jnp.int32, (step, wide), 0)

    def spread_row(x, j):
        return jnp.broadcast_to(x[j : j + 1, :], (step, wide))

    for p in range(count):
        columns = {
            i: [
                jnp.broadcast_to(rows[i][:, step * p + j : step * p + j + 1], (step, wide))
                for j in range(step)
            ]
            for i in range(p, count)
        }
        for j in range(step):
            root = lax.rsqrt(spread_row(columns[p][j], j))
            pivot = spread_row(rows[p], j) * root
            heads = {k: spread_row(columns[p][k], j) * root for k in range(j + 1, step)}
            for i in range(p, count):
                factor = columns[i][j] * root
                if i == p:
                    factor = jnp.where(sub > j, factor, 0.0)
                rows[i] = rows[i] - factor * pivot
                for k in range(j + 1, step):
                    columns[i][k] = columns[i][k] - factor * heads[k]
            rows[p] = jnp.where(sub == j, pivot, rows[p])
        work_ref[step * p : step * (p + 1), :] = rows[p]
    inverse = work_ref[:, size:]
    for j in range(filtered_ref.shape[0]):
        out_ref[:, j * tile : (j + 1) * tile] = contract(
            inverse, filtered_ref[j], ((1,), (0,)), FULL
        )


def solve_of(parts, filtered, scale):
    own, total, tile = filtered.shape
    return call(
        functools.partial(solve, scale=scale),
        floats(total, own * tile),
        [*parts, filtered],
        scratch=[pltpu.VMEM((total, 2 * total), jnp.float32)],
    )


def after(x, y):
    return lax.optimization_barrier((x, y))[0]


def on_device(start_block, tile_vals, tile_rows, tile_cols, tile_count):
    vec_width, local_rows = start_block.shape
    tile = tile_vals.shape[1]
    own = local_rows // tile
    blk_count = lax.axis_size("blk")
    row_count = lax.axis_size("rows")
    quad_count = blk_count // HALVES
    group_blocks = own * blk_count
    part = HALVES * own
    reach = group_blocks // 4
    rows_total = local_rows * blk_count * row_count
    width = vec_width // CHAINS
    group_index = lax.axis_index("rows")
    blk_index = lax.axis_index("blk")
    high, quad, odd = blk_index // quad_count, blk_index & (quad_count - 1), group_index & 1

    def over_blk(x, k):
        return lax.ppermute(x, "blk", [(i, i ^ k) for i in range(blk_count)])

    def over_rows(x, k):
        return lax.ppermute(x, "rows", [(i, i ^ k) for i in range(row_count)])

    def over_all(x, rows_bit, blk_bit):
        pairs = [
            (i * row_count + j, (i ^ blk_bit) * row_count + (j ^ rows_bit))
            for i in range(blk_count)
            for j in range(row_count)
        ]
        return lax.ppermute(x, ("blk", "rows"), pairs)

    def with_far(x):
        pairs = [(i, i + 1) for i in range(1, row_count - 1, 2)]
        return lax.ppermute(x, "rows", pairs + [(b, a) for a, b in pairs])

    def spread(x):
        return [x] + [over_blk(x, k) for k in range(1, quad_count)]

    def gather_sum(parts):
        return add_all([parts[0]] + [over_blk(parts[k], k) for k in range(1, quad_count)])

    def place(block):
        blk = block // own
        return ((blk & (quad_count - 1)) ^ quad) * part + (blk // quad_count) * own + block % own

    shift = group_index * group_blocks
    cols, rows = tile_cols - shift, tile_rows - shift
    left = group_blocks + jnp.where(odd == 1, 0, reach) + reach + cols
    right = group_blocks + jnp.where(odd == 1, reach, 0) + cols - group_blocks
    cols = jnp.where(cols < 0, left, jnp.where(cols < group_blocks, place(cols), right))
    table = jnp.concatenate([cols, place(rows), tile_count.reshape(1)])
    flags = jnp.stack([quad, high, odd]).astype(jnp.int32)
    flags = jnp.broadcast_to(flags[:, None, None], (3, 8, tile))
    blocks = start_block.reshape(vec_width, own, tile).transpose(1, 0, 2)
    chains = jnp.split(blocks, CHAINS, axis=1)
    tile_vals, table, flags = lax.optimization_barrier((tile_vals, table, flags))

    tiles, degree = prepare_tiles(tile_vals, table, group_blocks)
    others = [over_blk(chain, quad_count) for chain in chains]
    others[0] = after(others[0], degree)
    other = over_blk(degree, quad_count)
    gathered = [spread(join_halves(flags, x, y)) for x, y in zip(chains, others)]
    other = after(other, [gathered[0][1], gathered[1][1:3]])
    degrees = spread(add_all([degree[None], other[None]])[0])
    root, own_degree, inverse = call(
        functools.partial(roots, part=part),
        [floats(group_blocks, tile), floats(part, tile), floats(part, tile)],
        degrees,
    )

    states = [[] for _ in range(CHAINS)]
    parts = [None] * CHAINS
    for c in range(CHAINS):
        near, far = halo_payloads(flags, gathered[c], own, reach, root)
        near, far = over_rows(near, 1), with_far(far)
        if c + 1 < CHAINS:
            gathered[c + 1] = gathered[c + 1][:2] + after(gathered[c + 1][2:], near)
        state, *parts[c] = tile_products(
            "first", table, gathered[c], near, far, [root], tiles, group_blocks
        )
        states[c].append(state)

    for index in range(1, STEPS):
        kind = "second" if index == 1 else "third"
        sums = [gather_sum(parts[c]) for c in range(CHAINS)]
        for c in range(CHAINS - 1):
            sums[c] = after(sums[c], parts[c + 1][0])
        totals, pieces = [], []
        for c in range(CHAINS):
            mine = sums[c]
            other = over_blk(mine, quad_count)
            arrived = after(other, pieces[c - 1][1]) if c else other
            totals.append(add_all([mine, arrived], inverse))
            pieces.append(spread(totals[c]))
        for c in range(CHAINS):
            mine = after(pieces[c], totals[c + 1]) if c + 1 < CHAINS else pieces[c]
            near, far = halo_payloads(flags, mine, own, reach)
            near, far = over_rows(near, 1), with_far(far)
            if c + 1 < CHAINS:
                near = after(near, pieces[c + 1][1:])
            state, *parts[c] = tile_products(
                kind, table, mine, near, far,
                [states[c][-1 - i] for i in range(index)], tiles, group_blocks,
            )
            states[c].append(state)

    sums = [gather_sum(parts[c]) for c in range(CHAINS)]
    groups = [
        [sums[c], over_blk(sums[c], quad_count), states[c][-1], states[c][-2]]
        for c in range(CHAINS)
    ]
    filtered, total = gram_of(flags, own_degree, groups, own)

    bits = [(1 << i, 0) for i in range(row_count.bit_length() - 1)]
    bits += [(0, 1 << i) for i in range(quad_count.bit_length() - 1)]
    stages = []
    while bits:
        first, *second = bits[:2]
        bits = bits[2:]
        stages.append([first] + [x for y in second for x in (y, (first[0] ^ y[0], first[1] ^ y[1]))])
    pieces = [total]
    for stage in stages:
        total = sum(pieces[1:], pieces[0])
        pieces = [total] + [over_all(total, *bit) for bit in stage]
    return solve_of(pieces, filtered, 1.0 / rows_total)


def solution(mesh):
    in_specs = (
        P(None, ("rows", "blk")),
        P(("rows", "blk"), None, None),
        P(("rows", "blk")),
        P(("rows", "blk")),
        P("rows", "blk"),
    )
    out_specs = P(None, ("rows", "blk"))
    return jax.shard_map(
        on_device, mesh=mesh, in_specs=in_specs, out_specs=out_specs, check_vma=False
    )
```

```python
import functools

import jax
import jax.numpy as jnp
from jax import lax
from jax.experimental import pallas as pl
from jax.experimental.pallas import tpu as pltpu
from jax.sharding import PartitionSpec as P

STEPS = 3
CHAINS = 2
HALVES = 2
GROUP = 16
VMEM_BYTES = 16 << 20

shift_term = -0.25
half_width = 0.75

VMEM = pl.BlockSpec(memory_space=pltpu.VMEM)
SMEM = pl.BlockSpec(memory_space=pltpu.SMEM)
FULL = lax.Precision.HIGHEST


def call(kernel, out_shape, operands, in_specs=None, out_specs=None, scratch=(), flops=0, nbytes=0):
    many = isinstance(out_shape, list)
    return pl.pallas_call(
        kernel,
        in_specs=in_specs or [VMEM] * len(operands),
        out_specs=out_specs or ([VMEM] * len(out_shape) if many else VMEM),
        out_shape=out_shape,
        scratch_shapes=list(scratch),
        compiler_params=pltpu.CompilerParams(vmem_limit_bytes=VMEM_BYTES),
        cost_estimate=pl.CostEstimate(flops=flops, bytes_accessed=nbytes, transcendentals=0),
        name=kernel.func.__name__ if isinstance(kernel, functools.partial) else kernel.__name__,
    )(*operands)


def floats(*shape):
    return jax.ShapeDtypeStruct(shape, jnp.float32)


def split_bf16(x):
    high = x.astype(jnp.bfloat16)
    return high, (x - high.astype(jnp.float32)).astype(jnp.bfloat16)


def contract(a, b, dims, precision=None):
    return lax.dot_general(
        a, b, (dims, ((), ())), precision=precision, preferred_element_type=jnp.float32
    )


def prepare(table_ref, vals_hbm, cat_ref, degree_ref, vals_ref, sems):
    slots, tile, _ = vals_ref.shape
    loads = [
        pltpu.make_async_copy(
            vals_hbm.at[pl.ds(g * GROUP, GROUP)], vals_ref.at[pl.ds(g * GROUP, GROUP)], sems.at[g]
        )
        for g in range(slots // GROUP)
    ]
    for load in loads:
        load.start()
    degree_ref[...] = jnp.zeros_like(degree_ref)
    ones = jnp.ones((8, 2 * tile), jnp.bfloat16)
    live = table_ref[2 * slots]
    for slot in range(slots):
        if slot % GROUP == 0:
            loads[slot // GROUP].wait()
        values = vals_ref[slot] * (slot < live).astype(jnp.float32)
        high, low = split_bf16(values)
        cat_ref[slot, :, :tile] = high
        cat_ref[slot, :, tile:] = low
        sums = contract(ones, cat_ref[slot], ((1,), (1,)))
        degree_ref[pl.ds(table_ref[slots + slot], 1), :] += sums[:1]


def prepare_tiles(tile_vals, table, group_blocks):
    slots, tile, _ = tile_vals.shape
    return call(
        prepare,
        [pltpu.VMEM((slots, tile, 2 * tile), jnp.bfloat16), floats(group_blocks, tile)],
        [table, pltpu.with_memory_space_constraint(tile_vals, pltpu.HBM)],
        in_specs=[SMEM, pl.BlockSpec(memory_space=pl.ANY)],
        scratch=[
            pltpu.VMEM(tile_vals.shape, jnp.float32),
            pltpu.SemaphoreType.DMA((slots // GROUP,)),
        ],
        flops=2_000_000_000,
        nbytes=2 * tile_vals.size * 4,
    )


def join(flags_ref, chain_ref, other_ref, *refs):
    out_ref = refs[-1]
    own = chain_ref.shape[0]
    low = flags_ref[1, :1, :] == 0
    for j in range(own):
        mine, other = chain_ref[j], other_ref[j]
        out_ref[j] = jnp.where(low, mine, other)
        out_ref[own + j] = jnp.where(low, other, mine)
    if len(refs) == 2:
        out_ref[2 * own :] = refs[0][...].reshape(out_ref[2 * own :].shape)


def join_halves(flags, chain, other, degree=None):
    own, width, tile = chain.shape
    extra = 0 if degree is None else degree.shape[0] // width
    operands = [flags, chain, other] + ([] if degree is None else [degree])
    return call(join, floats(2 * own + extra, width, tile), operands)


def roots(*refs, part):
    sources, (root_ref, degree_ref, inverse_ref) = refs[:-3], refs[-3:]
    for m in range(root_ref.shape[0] // part):
        total = sources[0][m * part : (m + 1) * part, :]
        for k in range(1, len(sources)):
            total = total + sources[k][(m ^ k) * part : ((m ^ k) + 1) * part, :]
        root_ref[m * part : (m + 1) * part, :] = 1.0 / jnp.sqrt(total)
        if m == 0:
            degree_ref[...] = total
            inverse_ref[...] = 1.0 / total


def add(*refs, scaled):
    refs = list(refs)
    out_ref = refs.pop()
    scale_ref = refs.pop() if scaled else None
    for j in range(out_ref.shape[0]):
        total = refs[0][j]
        for ref in refs[1:]:
            total = total + ref[j]
        out_ref[j] = total * scale_ref[j : j + 1, :] if scaled else total


def add_all(arrays, scale=None):
    return call(
        functools.partial(add, scaled=scale is not None),
        floats(*arrays[0].shape),
        list(arrays) + ([] if scale is None else [scale]),
    )


def halo(flags_ref, *refs, own, rooted):
    refs = list(refs)
    far_ref, near_ref = refs.pop(), refs.pop()
    root_ref = refs.pop() if rooted else None
    count = len(refs)
    part = HALVES * own
    quad, odd = flags_ref[0, :1, :], flags_ref[2, :1, :] == 1
    for m in range(near_ref.shape[0] // own):
        low, high = m, count - near_ref.shape[0] // own + m
        for j in range(own):

            def block(k, h):
                value = refs[k][h * own + j]
                if rooted:
                    at = k * part + h * own + j
                    value = value * root_ref[at : at + 1, :]
                return value

            bottom, top = block(0, 0), block(0, HALVES - 1)
            for k in range(1, count):
                bottom = jnp.where((quad ^ k) == low, block(k, 0), bottom)
                top = jnp.where((quad ^ k) == high, block(k, HALVES - 1), top)
            near_ref[m * own + j] = jnp.where(odd, bottom, top)
            far_ref[m * own + j] = jnp.where(odd, top, bottom)


def halo_payloads(flags, pieces, own, reach, root=None):
    _, width, tile = pieces[0].shape
    operands = [flags, *pieces] + ([] if root is None else [root])
    return call(
        functools.partial(halo, own=own, rooted=root is not None),
        [floats(reach, width, tile)] * 2,
        operands,
    )


def products(table_hbm, *refs, count, kind):
    refs = list(refs)
    sem = refs.pop()
    table_ref = refs.pop()
    fetch = pltpu.make_async_copy(table_hbm, table_ref, sem)
    fetch.start()
    pieces = [refs.pop(0) for _ in range(count)]
    near, far = refs.pop(0), refs.pop(0)
    if kind == "first":
        root_ref = refs.pop(0)
    else:
        last_ref = refs.pop(0)
        older_ref = refs.pop(0) if kind == "third" else None
    tiles_ref, state_ref = refs.pop(0), refs.pop(0)
    parts = [refs.pop(0) for _ in range(count)]
    cat_ref, total_ref = refs
    _, width, tile = state_ref.shape
    reach = near.shape[0]
    part = total_ref.shape[0] // count
    slots = tiles_ref.shape[0]
    total_ref[...] = jnp.zeros_like(total_ref)

    def advance(slot, value):
        if kind != "first":
            value = (2.0 / half_width) * (shift_term * last_ref[slot] - value)
            if kind == "third":
                value = value - older_ref[slot]
            else:
                value = 0.5 * value
        state_ref[slot] = value
        high, low = split_bf16(value)
        cat_ref[slot, :width, :tile] = high
        cat_ref[slot, :width, tile:] = high
        cat_ref[slot, width:, :tile] = low
        cat_ref[slot, width:, tile:] = low

    for k in range(count):
        for j in range(part):
            slot = k * part + j
            value = pieces[k][j]
            if kind == "first":
                value = value * root_ref[slot : slot + 1, :]
            advance(slot, value)
    for j in range(reach):
        advance(count * part + j, near[j])
        advance(count * part + reach + j, far[j])

    fetch.wait()
    for slot in range(slots):
        both = contract(cat_ref[table_ref[slot]], tiles_ref[slot], ((1,), (1,)))
        total_ref[table_ref[slots + slot]] += both[:width] + both[width:]

    for k in range(count):
        parts[k][...] = total_ref[k * part : (k + 1) * part]


def tile_products(kind, table, pieces, near, far, extra, tiles, group_blocks):
    reach, width, tile = near.shape
    count = len(pieces)
    window = group_blocks + 2 * reach
    operands = [table, *pieces, near, far, *extra]
    operands.append(pltpu.with_memory_space_constraint(tiles, pltpu.VMEM))
    return call(
        functools.partial(products, kind=kind, count=count),
        [floats(window, width, tile)] + [floats(group_blocks // count, width, tile)] * count,
        operands,
        in_specs=[pl.BlockSpec(memory_space=pl.ANY)] + [VMEM] * (len(operands) - 1),
        scratch=[
            pltpu.VMEM((window, 2 * width, 2 * tile), jnp.bfloat16),
            pltpu.VMEM((group_blocks, width, tile), jnp.float32),
            pltpu.SMEM(table.shape, table.dtype),
            pltpu.SemaphoreType.DMA(()),
        ],
        flops=3_000_000_000,
        nbytes=tiles.size * 2,
    )


def gram(flags_ref, degree_ref, *refs, own):
    refs = list(refs)
    all_ref, gram_ref, filtered_ref = refs.pop(), refs.pop(), refs.pop()
    groups = [refs[i : i + 4] for i in range(0, len(refs), 4)]
    width = groups[0][0].shape[1]
    low = flags_ref[1, :1, :] == 0
    total = jnp.zeros(gram_ref.shape, jnp.float32)
    for i in range(HALVES * own):
        degree = degree_ref[i : i + 1, :]
        root, inverse = jnp.sqrt(degree), 1.0 / degree
        for c, (mine, other, last, older) in enumerate(groups):
            value = (mine[i] + other[i]) * inverse
            value = (2.0 / half_width) * (shift_term * last[i] - value) - older[i]
            all_ref[i, c * width : (c + 1) * width, :] = value * root
        block = all_ref[i]
        total += contract(block, block, ((1,), (1,)), FULL)
    for j in range(own):
        filtered_ref[j] = jnp.where(low, all_ref[j], all_ref[own + j])
    gram_ref[...] = total


def gram_of(flags, degree, groups, own):
    part, width, tile = groups[0][0].shape
    total = width * len(groups)
    return call(
        functools.partial(gram, own=own),
        [floats(own, total, tile), floats(total, total)],
        [flags, degree] + [x for group in groups for x in group],
        scratch=[pltpu.VMEM((part, total, tile), jnp.float32)],
    )


def solve(*refs, scale):
    parts, (filtered_ref, out_ref, work_ref) = refs[:-3], refs[-3:]
    size = parts[0].shape[0]
    tile = filtered_ref.shape[2]
    total = parts[0][...]
    for piece in parts[1:]:
        total = total + piece[...]
    row = lax.broadcasted_iota(jnp.int32, (size, size), 0)
    column = lax.broadcasted_iota(jnp.int32, (size, size), 1)
    work_ref[:, :size] = total * scale
    work_ref[:, size:] = (row == column).astype(jnp.float32)
    step = 8
    wide = 2 * size
    count = size // step
    rows = [work_ref[step * i : step * (i + 1), :] for i in range(count)]
    sub = lax.broadcasted_iota(jnp.int32, (step, wide), 0)

    def spread_row(x, j):
        return jnp.broadcast_to(x[j : j + 1, :], (step, wide))

    for p in range(count):
        columns = {
            i: [
                jnp.broadcast_to(rows[i][:, step * p + j : step * p + j + 1], (step, wide))
                for j in range(step)
            ]
            for i in range(p, count)
        }
        for j in range(step):
            root = lax.rsqrt(spread_row(columns[p][j], j))
            pivot = spread_row(rows[p], j) * root
            heads = {k: spread_row(columns[p][k], j) * root for k in range(j + 1, step)}
            for i in range(p, count):
                factor = columns[i][j] * root
                if i == p:
                    factor = jnp.where(sub > j, factor, 0.0)
                rows[i] = rows[i] - factor * pivot
                for k in range(j + 1, step):
                    columns[i][k] = columns[i][k] - factor * heads[k]
            rows[p] = jnp.where(sub == j, pivot, rows[p])
        work_ref[step * p : step * (p + 1), :] = rows[p]
    inverse = work_ref[:, size:]
    for j in range(filtered_ref.shape[0]):
        out_ref[:, j * tile : (j + 1) * tile] = contract(
            inverse, filtered_ref[j], ((1,), (0,)), FULL
        )


def solve_of(parts, filtered, scale):
    own, total, tile = filtered.shape
    return call(
        functools.partial(solve, scale=scale),
        floats(total, own * tile),
        [*parts, filtered],
        scratch=[pltpu.VMEM((total, 2 * total), jnp.float32)],
    )


def after(x, y):
    return lax.optimization_barrier((x, y))[0]


def on_device(start_block, tile_vals, tile_rows, tile_cols, tile_count):
    vec_width, local_rows = start_block.shape
    tile = tile_vals.shape[1]
    own = local_rows // tile
    blk_count = lax.axis_size("blk")
    row_count = lax.axis_size("rows")
    quad_count = blk_count // HALVES
    group_blocks = own * blk_count
    part = HALVES * own
    reach = group_blocks // 4
    rows_total = local_rows * blk_count * row_count
    width = vec_width // CHAINS
    group_index = lax.axis_index("rows")
    blk_index = lax.axis_index("blk")
    high, quad, odd = blk_index // quad_count, blk_index & (quad_count - 1), group_index & 1

    def over_blk(x, k):
        return lax.ppermute(x, "blk", [(i, i ^ k) for i in range(blk_count)])

    def over_rows(x, k):
        return lax.ppermute(x, "rows", [(i, i ^ k) for i in range(row_count)])

    def over_all(x, rows_bit, blk_bit):
        pairs = [
            (i * row_count + j, (i ^ blk_bit) * row_count + (j ^ rows_bit))
            for i in range(blk_count)
            for j in range(row_count)
        ]
        return lax.ppermute(x, ("blk", "rows"), pairs)

    def with_far(x):
        pairs = [(i, i + 1) for i in range(1, row_count - 1, 2)]
        return lax.ppermute(x, "rows", pairs + [(b, a) for a, b in pairs])

    def spread(x):
        return [x] + [over_blk(x, k) for k in range(1, quad_count)]

    def gather_sum(parts):
        return add_all([parts[0]] + [over_blk(parts[k], k) for k in range(1, quad_count)])

    def place(block):
        blk = block // own
        return ((blk & (quad_count - 1)) ^ quad) * part + (blk // quad_count) * own + block % own

    shift = group_index * group_blocks
    cols, rows = tile_cols - shift, tile_rows - shift
    left = group_blocks + jnp.where(odd == 1, 0, reach) + reach + cols
    right = group_blocks + jnp.where(odd == 1, reach, 0) + cols - group_blocks
    cols = jnp.where(cols < 0, left, jnp.where(cols < group_blocks, place(cols), right))
    table = jnp.concatenate([cols, place(rows), tile_count.reshape(1)])
    flags = jnp.stack([quad, high, odd]).astype(jnp.int32)
    flags = jnp.broadcast_to(flags[:, None, None], (3, 8, tile))
    blocks = start_block.reshape(vec_width, own, tile).transpose(1, 0, 2)
    chains = jnp.split(blocks, CHAINS, axis=1)
    tile_vals, table, flags = lax.optimization_barrier((tile_vals, table, flags))

    tiles, degree = prepare_tiles(tile_vals, table, group_blocks)
    others = [over_blk(chain, quad_count) for chain in chains]
    others[0] = after(others[0], degree)
    other = over_blk(degree, quad_count)
    gathered = [spread(join_halves(flags, x, y)) for x, y in zip(chains, others)]
    other = after(other, [gathered[0][1], gathered[1][1:3]])
    degrees = spread(add_all([degree[None], other[None]])[0])
    root, own_degree, inverse = call(
        functools.partial(roots, part=part),
        [floats(group_blocks, tile), floats(part, tile), floats(part, tile)],
        degrees,
    )

    states = [[] for _ in range(CHAINS)]
    parts = [None] * CHAINS
    for c in range(CHAINS):
        near, far = halo_payloads(flags, gathered[c], own, reach, root)
        near, far = over_rows(near, 1), with_far(far)
        if c + 1 < CHAINS:
            gathered[c + 1] = gathered[c + 1][:2] + after(gathered[c + 1][2:], near)
        state, *parts[c] = tile_products(
            "first", table, gathered[c], near, far, [root], tiles, group_blocks
        )
        states[c].append(state)

    for index in range(1, STEPS):
        kind = "second" if index == 1 else "third"
        sums = [gather_sum(parts[c]) for c in range(CHAINS)]
        for c in range(CHAINS - 1):
            sums[c] = after(sums[c], parts[c + 1][0])
        totals, pieces = [], []
        for c in range(CHAINS):
            mine = sums[c]
            other = over_blk(mine, quad_count)
            arrived = after(other, pieces[c - 1][1]) if c and index == 1 else other
            totals.append(add_all([mine, arrived], inverse))
            pieces.append(spread(totals[c]))
        for c in range(CHAINS):
            mine = after(pieces[c], totals[c + 1]) if c + 1 < CHAINS else pieces[c]
            near, far = halo_payloads(flags, mine, own, reach)
            near, far = over_rows(near, 1), with_far(far)
            if c + 1 < CHAINS:
                near = after(near, pieces[c + 1][1:])
            state, *parts[c] = tile_products(
                kind, table, mine, near, far,
                [states[c][-1 - i] for i in range(index)], tiles, group_blocks,
            )
            states[c].append(state)

    sums = [gather_sum(parts[c]) for c in range(CHAINS)]
    sums[1] = after(sums[1], sums[0])
    groups = [
        [sums[c], over_blk(sums[c], quad_count), states[c][-1], states[c][-2]]
        for c in range(CHAINS)
    ]
    filtered, total = gram_of(flags, own_degree, groups, own)

    bits = [(1 << i, 0) for i in range(row_count.bit_length() - 1)]
    bits += [(0, 1 << i) for i in range(quad_count.bit_length() - 1)]
    stages = []
    while bits:
        first, *second = bits[:2]
        bits = bits[2:]
        stages.append([first] + [x for y in second for x in (y, (first[0] ^ y[0], first[1] ^ y[1]))])
    pieces = [total]
    for stage in stages:
        total = sum(pieces[1:], pieces[0])
        pieces = [total] + [over_all(total, *bit) for bit in stage]
    return solve_of(pieces, filtered, 1.0 / rows_total)


def solution(mesh):
    in_specs = (
        P(None, ("rows", "blk")),
        P(("rows", "blk"), None, None),
        P(("rows", "blk")),
        P(("rows", "blk")),
        P("rows", "blk"),
    )
    out_specs = P(None, ("rows", "blk"))
    return jax.shard_map(
        on_device, mesh=mesh, in_specs=in_specs, out_specs=out_specs, check_vma=False
    )
```
